128 devices in a mesh: frag: 64 (over z, y, x), inner: 2 (over core).
Axes of the slice: x: 4, y: 4, z: 4, core: 2. Of those that a mesh axis runs over, the one named last changes fastest.
Arguments:
- density: bfloat16 [4096, 256, 256], P('frag', 'inner'), may hold values from -6 to 6
- core_hamiltonian: bfloat16 [4096, 256, 256], P('frag', 'inner'), may hold values from -6 to 6
- coulomb_kernel: bfloat16 [4096, 256, 256], P('frag', 'inner'), may hold values from -0.375 to 0.375
- esp_kernel: bfloat16 [4096, 256, 256], P('frag', 'inner'), may hold values from -0.375 to 0.375
- contacts: int32 [4096, 16], replicated, may hold values from -1 to 4095, as said below
- coupling: float32 [4096, 16], P('frag'), may hold values from 0.1 to 1
- partner: int32 [4096], P('frag'), may hold values from 0 to 4095, as said below
Outputs:
- fock: bfloat16 [4096, 256, 256], P(('frag', 'inner'))
- new_density: bfloat16 [4096, 256, 256], P(('frag', 'inner'))
- partner_energy: float32 [4096], P('frag')
The draws below stay inside these ranges and needn't reach their ends.
Inputs may be any that keep to these rules, and one draw needn't show every extreme that they name: `contacts`: -1 marks an empty slot. No fragment names itself. Taking groups of 64 fragments in order, a named fragment lies in a group at most 2 groups away from the naming one. At most 4 contact slots of one group name fragments of any one other group (several slots may name the same fragment), and every group has exactly 4 slots naming fragments of some one other group. Taking groups of 64 fragments in order, the partner of a fragment in group 2m lies in group 2m + 1 and the reverse; the partner of a fragment's partner is the fragment itself.
All inputs are finite; a program needn't handle non-finite values.
Results may differ from the reference program's by a relative error of at most 0.009.
The reference program's roundings to bfloat16 on the way count: a program that leaves them out, or rounds other values in their place, can miss the bound.
Values may be sent and summed in bfloat16 or wider, within the bound.
No kernel may reach another device: no remote copies, remote signals or barrier semaphores. Data moves between devices by JAX's collectives and lax.ppermute only.
A program may use at most 192 MiB of HBM per device.

```python
import math
import jax
import jax.numpy as jnp
from jax import lax

NB = 256
FG = 64
NN = 16
CAPG = 4
RG = 2
NPUR = 6
NFRAG = 4096


def draw_contacts(key, part):
    groups = NFRAG // FG
    places = FG * NN
    offsets = [direction * distance for distance in range(1, RG + 1) for direction in (1, -1)]
    move_count = len(offsets)
    subkeys = jax.random.split(key, 6)
    home_group = jnp.arange(groups, dtype=jnp.int32)[:, None]
    offset_row = jnp.array(offsets, dtype=jnp.int32)[None, :]
    in_range = (home_group + offset_row >= 0) & (home_group + offset_row < groups)
    counts = jax.random.randint(subkeys[0], (groups, move_count), 1, CAPG + 1)
    scores = jax.random.randint(subkeys[1], (groups, move_count), 0, 1000) * move_count + jnp.arange(move_count)[None, :]
    scores = jnp.where(in_range, scores, -1)
    forced = jnp.argmax(scores, axis=1)
    counts = jnp.where(jnp.arange(move_count)[None, :] == forced[:, None], CAPG, counts)
    counts = jnp.where(in_range, counts, 0)
    limits = jnp.cumsum(counts, axis=1)

    def shuffle_group(subkey):
        return jax.random.permutation(subkey, places)
    shuffled = jax.vmap(shuffle_group)(jax.random.split(subkeys[2], groups))
    positions = jnp.argsort(shuffled, axis=1)
    slot_class = jnp.sum(positions[:, :, None] >= limits[:, None, :], axis=2)
    class_offset = jnp.concatenate([offset_row[0], jnp.zeros((1,), jnp.int32)])
    step_group = home_group + class_offset[slot_class]
    remote = slot_class < move_count
    far_place = jax.random.randint(subkeys[3], (groups, places), 0, FG)
    own_place = (jnp.arange(places) // NN)[None, :]
    near_place = (own_place + 1 + jax.random.randint(subkeys[4], (groups, places), 0, FG - 1)) % FG
    unused = jax.random.randint(subkeys[5], (groups, places), 0, 4) == 0
    named = jnp.where(remote, step_group * FG + far_place, jnp.where(unused, -1, home_group * FG + near_place))
    return named.reshape(NFRAG, NN).astype(jnp.int32)


def draw_partner(key, part):
    groups = NFRAG // FG
    pair_count = groups // 2

    def shuffle_pair(subkey):
        return jax.random.permutation(subkey, FG)
    orders = jax.vmap(shuffle_pair)(jax.random.split(key, pair_count)).astype(jnp.int32)
    inverse = jnp.argsort(orders, axis=1).astype(jnp.int32)
    pair_base = jnp.arange(pair_count, dtype=jnp.int32)[:, None] * (2 * FG)
    even_side = pair_base + FG + orders
    odd_side = pair_base + inverse
    return jnp.stack([even_side, odd_side], axis=1).reshape(NFRAG).astype(jnp.int32)


def block_scale(stream_key, shape, shards, least, high):
    gain, own = 1.0, jax.random.fold_in(stream_key, 6)
    for position, shards_of in shards:
        draws = jnp.exp(jax.random.uniform(jax.random.fold_in(own, position), (shards_of,), jnp.float32, least / len(shards), high / len(shards)))
        gain = gain * jnp.repeat(draws, shape[position] // shards_of).reshape([-1 if axis == position else 1 for axis in range(len(shape))])
    return gain


def normal_values(stream_key, dims, scale, bound, shards=(), kind=jnp.bfloat16):
    factor_of = block_scale(stream_key, dims, shards, -0.22, 0.18) if shards else 1.0
    values = jax.random.normal(stream_key, dims, jnp.float32) * scale * factor_of
    return jnp.minimum(jnp.maximum(values, -bound), bound).astype(kind)


def setup_inputs(seed: int = 0) -> dict:
    seeds = jax.random.split(jax.random.key(seed), 8)
    density = normal_values(seeds[0], (NFRAG, NB, NB), 1.0, 6.0, ((0, 64), (1, 2)))
    core_hamiltonian = normal_values(seeds[1], (NFRAG, NB, NB), 1.0, 6.0, ((0, 64), (1, 2)))
    coulomb_kernel = normal_values(seeds[2], (NFRAG, NB, NB), NB ** -0.5, 0.375, ((0, 64), (1, 2)))
    esp_kernel = normal_values(seeds[3], (NFRAG, NB, NB), NB ** -0.5, 0.375, ((0, 64), (1, 2)))
    contacts = draw_contacts(jax.random.fold_in(seeds[7], 71), 0)
    coupling = jnp.clip(jnp.exp(math.log(1.0) - 2.3025851 * jax.random.uniform(seeds[5], (NFRAG, NN), jnp.float32) ** block_scale(seeds[5], (NFRAG, NN), ((0, 64),), -0.2, 0.2)), 0.1, 1.0)
    partner = draw_partner(jax.random.fold_in(seeds[7], 71), 0)
    return {"density": density, "core_hamiltonian": core_hamiltonian, "coulomb_kernel": coulomb_kernel, "esp_kernel": esp_kernel, "contacts": contacts, "coupling": coupling, "partner": partner}


def batched(left, right):
    return jnp.einsum('fab,fbc->fac', left.astype(jnp.float32), right.astype(jnp.float32), precision=lax.Precision.HIGHEST)

def purify(fock_group):
    wide = fock_group.astype(jnp.float32)
    symmetric = 0.5 * (wide + jnp.swapaxes(wide, 1, 2))
    identity = jnp.eye(NB, dtype=jnp.float32)
    centre = jnp.trace(symmetric, axis1=1, axis2=2) / NB
    centred = symmetric - centre[:, None, None] * identity
    spread = jnp.sqrt(lax.optimization_barrier(jnp.sum(centred * centred, axis=(1, 2))) + 1e-06)
    estimate = (0.5 * identity - centred / (2.0 * spread[:, None, None])).astype(jnp.bfloat16)
    for iteration in range(NPUR):
        square = batched(estimate, estimate).astype(jnp.bfloat16)
        cube_term = batched(square, estimate)
        estimate = (3.0 * square.astype(jnp.float32) - 2.0 * cube_term).astype(jnp.bfloat16)
    return estimate

def build_terms(inputs):
    densities, kernels, responses = inputs
    esp_image = batched(kernels, densities).astype(jnp.bfloat16)
    return (esp_image, batched(responses, densities))

def reference(density, core_hamiltonian, coulomb_kernel, esp_kernel, contacts, coupling, partner):
    groups = NFRAG // FG

    def regroup(array):
        return array.reshape(groups, FG, NB, NB)
    esp_image, coulomb = lax.map(build_terms, (regroup(density), regroup(esp_kernel), regroup(coulomb_kernel)))
    esp_image = esp_image.reshape(NFRAG, NB, NB)
    coulomb = coulomb.reshape(NFRAG, NB, NB)
    source_group = jnp.arange(NFRAG) // FG
    image_wide = esp_image.astype(jnp.float32)

    def add_slot(potential, inputs):
        targets, weights = inputs
        esp_block = weights[:, None, None] * image_wide
        rounded = lax.optimization_barrier(esp_block.astype(jnp.bfloat16)).astype(jnp.float32)
        remote = (targets >= 0) & (targets // FG != source_group)
        esp_block = jnp.where(remote[:, None, None], rounded, esp_block)
        target_row = jnp.where(targets >= 0, targets, NFRAG)
        return (potential.at[target_row].add(esp_block, mode='drop'), None)
    potential, ignored = lax.scan(add_slot, jnp.zeros((NFRAG, NB, NB), jnp.float32), (contacts.T, coupling.T))
    fock = (core_hamiltonian.astype(jnp.float32) + coulomb + potential).astype(jnp.bfloat16)
    partner_density = density[partner]
    partner_energy = lax.optimization_barrier(jnp.sum(partner_density.astype(jnp.float32) * image_wide, axis=(1, 2))) / NB
    new_density = lax.map(purify, regroup(fock)).reshape(NFRAG, NB, NB)
    return (fock, new_density, partner_energy)
```

```python
import functools

import jax
import jax.numpy as jnp
from jax import lax
from jax.experimental import pallas as pl
from jax.experimental.pallas import tpu as pltpu
from jax.sharding import PartitionSpec as P

NN = 16
CAPG = 4
NPUR = 6
OFFSETS = (1, -1, 2, -2)
SLOTS = len(OFFSETS) * CAPG
LOCAL_STEP = 4
ROW_STEP = 16
PURE_STEP = 4
ENERGY_STEP = 4
NONE = float(1 << 20)
SMEM = pl.BlockSpec(memory_space=pltpu.SMEM)
F32 = jnp.float32
BF16 = jnp.bfloat16


def dot(left, right):
    return jnp.dot(left, right, preferred_element_type=F32)


def params(mib=48):
    return pltpu.CompilerParams(vmem_limit_bytes=mib << 20)


def index_kernel(own_ref, low_ref, mid_ref, high_ref, coupling_ref, weight_ref, partner_ref, meta_ref, sent_ref, local_ref):
    own = own_ref[0]
    lists = jnp.concatenate([low_ref[...], mid_ref[...], high_ref[...]], axis=1)
    slot = lax.broadcasted_iota(jnp.int32, lists.shape, 0)
    lane = lax.broadcasted_iota(jnp.int32, lists.shape, 1)
    source = (own // 2 - 1) * 2 + (lane >> 6)
    target = lists >> 6
    key = (((slot * 64 + (lane & 63)) << 6) + (lists & 63)).astype(F32)
    leaving, arriving = [], []
    for offset in OFFSETS:
        leaving.append(jnp.where((source == own) & (target == own + offset), key, NONE))
        giver = own - offset
        giver = jnp.where((giver >= 0) & (giver < 64), giver, -999)
        arriving.append(jnp.where((source == giver) & (target == own), key, NONE))
    for rank in range(CAPG):
        for place in range(len(OFFSETS)):
            at = place * CAPG + rank
            least = jnp.min(leaving[place])
            leaving[place] = jnp.where(leaving[place] > least, leaving[place], NONE)
            code = jnp.where(least < NONE, least, 0.0).astype(jnp.int32)
            fragment = (code >> 6) & 63
            meta_ref[at] = fragment
            sent_ref[at] = weight_ref[code >> 12, fragment]
            least = jnp.min(arriving[place])
            arriving[place] = jnp.where(arriving[place] > least, arriving[place], NONE)
            code = jnp.where(least < NONE, least, -1.0).astype(jnp.int32)
            meta_ref[SLOTS + at] = jnp.where(code >= 0, code & 63, -1)

    def invert(step, carry):
        meta_ref[2 * SLOTS + (partner_ref[step] & 63)] = step
        return carry

    lax.fori_loop(0, 64, invert, 0)
    middle = mid_ref[...]
    half = lax.broadcasted_iota(jnp.int32, middle.shape, 1) >> 6
    middle = jnp.where(half == own % 2, middle - own * 64, -1)
    coupling = jnp.concatenate([coupling_ref[...], coupling_ref[...]], axis=1)
    row = lax.broadcasted_iota(jnp.int32, (64, 128), 0)
    wide = jnp.zeros((64, 128), F32)
    for k in range(NN):
        wide = wide + jnp.where(middle[k : k + 1] == row, coupling[k : k + 1], 0.0)
    weights = wide[:, :64] + wide[:, 64:]
    first = weights.astype(BF16)
    rest = weights - first.astype(F32)
    second = rest.astype(BF16)
    local_ref[:, 0:64] = first
    local_ref[:, 64:128] = second
    local_ref[:, 128:192] = (rest - second.astype(F32)).astype(BF16)


def make_index(own, contacts, coupling, partner):
    def block(shift):
        return pl.BlockSpec((NN, 128), lambda i, s: (0, jnp.clip(s[0] // 2 + shift, 0, 31)))

    return pl.pallas_call(
        index_kernel,
        grid_spec=pltpu.PrefetchScalarGridSpec(
            num_scalar_prefetch=1,
            grid=(1,),
            in_specs=[block(-1), block(0), block(1), pl.BlockSpec((NN, 64), lambda i, s: (0, 0)), SMEM, SMEM],
            out_specs=[SMEM, SMEM, pl.BlockSpec((64, 192), lambda i, s: (0, 0))],
        ),
        out_shape=[
            jax.ShapeDtypeStruct((2 * SLOTS + 64,), jnp.int32),
            jax.ShapeDtypeStruct((SLOTS,), F32),
            jax.ShapeDtypeStruct((64, 192), BF16),
        ],
        name="slots",
    )(own, contacts, contacts, contacts, coupling, coupling, partner)


def assemble(whole, inner, own, other):
    whole[pl.ds(pl.multiple_of(inner * 128, 128), 128), :] = own
    whole[pl.ds(pl.multiple_of(128 - inner * 128, 128), 128), :] = other


def outgoing_kernel(meta_ref, inner_ref, sent_ref, *refs):
    count = len(OFFSETS)
    kernels, own, other, outs, whole = (
        refs[:count], refs[count : 2 * count], refs[2 * count : 3 * count], refs[3 * count : 4 * count], refs[-1]
    )
    step = pl.program_id(0)
    for place in range(count):
        assemble(whole.at[place], inner_ref[0], own[place][0], other[place][0])
        image = dot(kernels[place][0], whole[place]).astype(BF16)
        weight = sent_ref[place * CAPG + step]
        outs[place][0] = (image.astype(F32) * weight).astype(BF16)


def make_outgoing(meta, inner, sent, esp_kernel, density, other):
    count = len(OFFSETS)

    def block(place):
        return pl.BlockSpec((1, 128, 256), lambda c, m, i: (m[place * CAPG + c], 0, 0))

    blocks = [block(place) for place in range(count)]
    return pl.pallas_call(
        outgoing_kernel,
        grid_spec=pltpu.PrefetchScalarGridSpec(
            num_scalar_prefetch=2,
            grid=(CAPG,),
            in_specs=[SMEM] + blocks * 3,
            out_specs=[pl.BlockSpec((1, 128, 256), lambda c, m, i: (c, 0, 0))] * count,
            scratch_shapes=[pltpu.VMEM((count, 256, 256), BF16)],
        ),
        out_shape=[jax.ShapeDtypeStruct((CAPG, 128, 256), BF16)] * count,
        compiler_params=params(),
        cost_estimate=pl.CostEstimate(flops=16 * 2 * 128 * 256 * 256, bytes_accessed=4 << 20, transcendentals=0),
        name="outgoing",
    )(meta, inner, sent, *[esp_kernel] * count, *[density] * count, *[other] * count)


def local_kernel(inner_ref, own, other, esp, response, core, weights, image_out, sum_out, wide, sums, whole):
    step = pl.program_id(0)
    loads = 64 // LOCAL_STEP

    @pl.when(step < loads)
    def _():
        for f in range(LOCAL_STEP):
            assemble(whole.at[f], inner_ref[0], own[f], other[f])
            both = jnp.concatenate([esp[f], response[f]], axis=0)
            result = dot(both, whole[f])
            image = result[:128].astype(BF16)
            image_out[f] = image
            rows = pl.ds(pl.multiple_of((step * LOCAL_STEP + f) * 128, 128), 128)
            image = image.astype(F32)
            total = result[128:] + core[f].astype(F32)
            for side in range(2):
                wide[side, rows, :] = image[:, side * 128 : side * 128 + 128]
                sums[side, rows, :] = total[:, side * 128 : side * 128 + 128]

    @pl.when(step >= loads)
    def _():
        matrix = weights[...]
        base = (step - loads) * ROW_STEP
        out = sum_out
        for r in range(ROW_STEP):
            at = pl.ds(base + r, 64, stride=128)
            tile = jnp.concatenate([wide[0, at, :], wide[1, at, :]], axis=1).astype(BF16)
            mixed = dot(matrix, jnp.concatenate([tile, tile, tile], axis=0))
            for side in range(2):
                out[side, pl.ds(r, 64, stride=ROW_STEP), :] = (
                    mixed[:, side * 128 : side * 128 + 128] + sums[side, at, :]
                )


def make_local(inner, density, other, esp_kernel, coulomb_kernel, core_hamiltonian, weights):
    loads, rows = 64 // LOCAL_STEP, 128 // ROW_STEP
    block = pl.BlockSpec((LOCAL_STEP, 128, 256), lambda t, i: (jnp.minimum(t, loads - 1), 0, 0))
    return pl.pallas_call(
        local_kernel,
        grid_spec=pltpu.PrefetchScalarGridSpec(
            num_scalar_prefetch=1,
            grid=(loads + rows,),
            in_specs=[block] * 5 + [pl.BlockSpec((64, 192), lambda t, i: (0, 0))],
            out_specs=[block, pl.BlockSpec((2, 64 * ROW_STEP, 128), lambda t, i: (0, jnp.maximum(t - loads, 0), 0))],
            scratch_shapes=[
                pltpu.VMEM((2, 64 * 128, 128), F32),
                pltpu.VMEM((2, 64 * 128, 128), F32),
                pltpu.VMEM((LOCAL_STEP, 256, 256), BF16),
            ],
        ),
        out_shape=[
            jax.ShapeDtypeStruct((64, 128, 256), BF16),
            jax.ShapeDtypeStruct((2, rows * 64 * ROW_STEP, 128), F32),
        ],
        compiler_params=params(),
        cost_estimate=pl.CostEstimate(flops=64 * 2 * 256 * 256 * 256, bytes_accessed=32 << 20, transcendentals=0),
        name="local",
    )(inner, density, other, esp_kernel, coulomb_kernel, core_hamiltonian, weights)


def fock_kernel(meta_ref, first_ref, sums, *refs):
    arrived, out, total = refs[:-2], refs[-2], refs[-1]
    step = pl.program_id(0)
    count = out.shape[0]
    for side in range(2):
        total[:, :, side * 128 : side * 128 + 128] = jnp.concatenate(
            [sums[side, tile].reshape(count, ROW_STEP, 128) for tile in range(128 // ROW_STEP)], axis=1
        )
    start = first_ref[0] + step * count
    for slot in range(SLOTS):
        place = meta_ref[SLOTS + slot] - start

        @pl.when((place >= 0) & (place < count))
        def _(slot=slot, place=place):
            total[place] += arrived[slot // CAPG][slot % CAPG].astype(F32)

    out[...] = total[...].astype(BF16)


def make_fock(meta, first, sums, arrived, number, count=8):
    tiles = 128 // ROW_STEP
    blocked = sums.reshape(2, tiles, 64 * ROW_STEP, 128)
    whole = pl.BlockSpec((CAPG, 128, 256), lambda t, m, f: (0, 0, 0))
    return pl.pallas_call(
        fock_kernel,
        grid_spec=pltpu.PrefetchScalarGridSpec(
            num_scalar_prefetch=2,
            grid=(number // count,),
            in_specs=[pl.BlockSpec((2, tiles, count * ROW_STEP, 128), lambda t, m, f: (0, 0, f[0] // count + t, 0))]
            + [whole] * len(OFFSETS),
            out_specs=pl.BlockSpec((count, 128, 256), lambda t, m, f: (t, 0, 0)),
            scratch_shapes=[pltpu.VMEM((count, 128, 256), F32)],
        ),
        out_shape=jax.ShapeDtypeStruct((number, 128, 256), BF16),
        compiler_params=params(),
        cost_estimate=pl.CostEstimate(flops=1 << 22, bytes_accessed=number * 3 << 16, transcendentals=0),
        name="fock_rows",
    )(meta, first, blocked, *arrived)


def pure_kernel(inner_ref, own, other, fock_out, density_out):
    row = lax.broadcasted_iota(jnp.int32, (256, 256), 0)
    column = lax.broadcasted_iota(jnp.int32, (256, 256), 1)
    diagonal = row == column
    identity = diagonal.astype(F32)
    turn = identity.astype(BF16)
    estimates = []
    for f in range(PURE_STEP):
        assemble(fock_out.at[f], inner_ref[0], own[f], other[f])
    for f in range(PURE_STEP):
        rows = fock_out[f]
        turned = lax.dot_general(turn, rows, (((1,), (1,)), ((), ())), preferred_element_type=F32)
        symmetric = 0.5 * (rows.astype(F32) + turned)
        centre = jnp.sum(jnp.where(diagonal, symmetric, 0.0), axis=(0, 1), keepdims=True) * (1.0 / 256)
        centred = symmetric - centre * identity
        spread = jnp.sqrt(jnp.sum(centred * centred, axis=(0, 1), keepdims=True) + 1e-6)
        estimates.append((0.5 * identity - centred * (0.5 / spread)).astype(BF16))
    for iteration in range(NPUR):
        squares = [dot(e, e).astype(BF16) for e in estimates]
        cubes = [dot(s, e) for s, e in zip(squares, estimates)]
        estimates = [(3.0 * s.astype(F32) - 2.0 * c).astype(BF16) for s, c in zip(squares, cubes)]
    for f in range(PURE_STEP):
        density_out[f] = estimates[f]


def make_pure(inner, own, other):
    number = own.shape[0]
    rows = pl.BlockSpec((PURE_STEP, 128, 256), lambda t, i: (t, 0, 0))
    whole = pl.BlockSpec((PURE_STEP, 256, 256), lambda t, i: (t, 0, 0))
    return pl.pallas_call(
        pure_kernel,
        grid_spec=pltpu.PrefetchScalarGridSpec(
            num_scalar_prefetch=1,
            grid=(number // PURE_STEP,),
            in_specs=[rows, rows],
            out_specs=[whole, whole],
        ),
        out_shape=[jax.ShapeDtypeStruct((number, 256, 256), BF16)] * 2,
        compiler_params=params(),
        cost_estimate=pl.CostEstimate(flops=number * 13 * 2 * 256**3, bytes_accessed=number * 3 << 17, transcendentals=0),
        name="purify",
    )(inner, own, other)


def energy_kernel(meta_ref, first, swapped, *refs):
    images, out = refs[:-1], refs[-1]
    step = pl.program_id(0)

    @pl.when(step == 0)
    def _():
        out[...] = jnp.zeros_like(out)

    for f in range(ENERGY_STEP):
        product = swapped[f].astype(F32) * images[f][0].astype(F32)
        line = jnp.sum(product, axis=0, keepdims=True)
        place = meta_ref[2 * SLOTS + first + step * ENERGY_STEP + f]
        out[pl.ds(place, 1), :] = line[:, :128] + line[:, 128:]


def make_energy(meta, first, swapped, image):
    number = swapped.shape[0]

    def block(f):
        return pl.BlockSpec((1, 128, 256), lambda t, m: (m[2 * SLOTS + first + t * ENERGY_STEP + f], 0, 0))

    return pl.pallas_call(
        lambda meta_ref, *refs: energy_kernel(meta_ref, first, *refs),
        grid_spec=pltpu.PrefetchScalarGridSpec(
            num_scalar_prefetch=1,
            grid=(number // ENERGY_STEP,),
            in_specs=[pl.BlockSpec((ENERGY_STEP, 128, 256), lambda t, m: (t, 0, 0))]
            + [block(f) for f in range(ENERGY_STEP)],
            out_specs=pl.BlockSpec((64, 128), lambda t, m: (0, 0)),
        ),
        out_shape=jax.ShapeDtypeStruct((64, 128), F32),
        cost_estimate=pl.CostEstimate(flops=number << 16, bytes_accessed=number << 17, transcendentals=0),
        name="energy",
    )(meta, swapped, *[image] * ENERGY_STEP)


def along(array, axis, by):
    length = lax.axis_size(axis)
    return lax.ppermute(array, axis, [(i, i + by) for i in range(length) if 0 <= i + by < length])


def exchanged(array, axis):
    return lax.ppermute(array, axis, [(i, i ^ 1) for i in range(lax.axis_size(axis))])


CUTS = (0, 48, 64)


def body(density, core_hamiltonian, coulomb_kernel, esp_kernel, contacts, coupling, partner):
    own = lax.axis_index("frag").astype(jnp.int32).reshape(1)
    inner = lax.axis_index("inner").astype(jnp.int32).reshape(1)
    other = exchanged(density, "inner")
    swapped = [exchanged(density[a:b], "frag") for a, b in zip(CUTS, CUTS[1:])]
    meta, sent, weights = make_index(own, contacts.T, coupling.T, partner)
    outgoing = make_outgoing(meta, inner, sent, esp_kernel, density, other)
    arrived = [along(block, "frag", by) for block, by in zip(outgoing, OFFSETS)]
    image, sums = make_local(inner, density, other, esp_kernel, coulomb_kernel, core_hamiltonian, weights)
    leave = make_fock(meta, 32 - inner * 32, sums, arrived, 32)
    stay = make_fock(meta, inner * 32, sums, arrived, 32)
    came = exchanged(leave, "inner")
    fock, new_density = make_pure(inner, stay, came)
    lines = sum(make_energy(meta, a, part, image) for a, part in zip(CUTS, swapped))
    energy = lax.psum(jnp.sum(lines, axis=1) * (1.0 / 256), "inner")
    return (fock, new_density, energy)


def solution(mesh):
    rows = P("frag", "inner", None)
    whole = P(("frag", "inner"), None, None)
    return jax.shard_map(
        body,
        mesh=mesh,
        in_specs=(rows, rows, rows, rows, P(), P("frag", None), P("frag")),
        out_specs=(whole, whole, P("frag")),
        check_vma=False,
    )
```

```python
import functools

import jax
import jax.numpy as jnp
from jax import lax
from jax.experimental import pallas as pl
from jax.experimental.pallas import tpu as pltpu
from jax.sharding import PartitionSpec as P

NN = 16
CAPG = 4
NPUR = 6
OFFSETS = (1, -1, 2, -2)
SLOTS = len(OFFSETS) * CAPG
LOCAL_STEP = 8
ROW_STEP = 8
PITCH = 136
PURE_STEP = 8
ENERGY_STEP = 8
FIRST = 24
SECOND = 32
ANY = pl.BlockSpec(memory_space=pl.ANY)
NONE = float(1 << 20)
SMEM = pl.BlockSpec(memory_space=pltpu.SMEM)
SMALL = pl.CostEstimate(flops=1 << 16, bytes_accessed=1 << 12, transcendentals=0)
F32 = jnp.float32
BF16 = jnp.bfloat16


def dot(left, right):
    return jnp.dot(left, right, preferred_element_type=F32)


def params(mib):
    return pltpu.CompilerParams(vmem_limit_bytes=mib << 20)


def index_kernel(own_ref, low_ref, mid_ref, high_ref, coupling_ref, weight_ref, partner_ref, meta_ref, sent_ref, local_ref):
    own = own_ref[0]
    lists = jnp.concatenate([low_ref[...], mid_ref[...], high_ref[...]], axis=1)
    slot = lax.broadcasted_iota(jnp.int32, lists.shape, 0)
    lane = lax.broadcasted_iota(jnp.int32, lists.shape, 1)
    source = (own // 2 - 1) * 2 + (lane >> 6)
    target = lists >> 6
    key = (((slot * 64 + (lane & 63)) << 6) + (lists & 63)).astype(F32)
    leaving, arriving = [], []
    for offset in OFFSETS:
        leaving.append(jnp.where((source == own) & (target == own + offset), key, NONE))
        giver = own - offset
        giver = jnp.where((giver >= 0) & (giver < 64), giver, -999)
        arriving.append(jnp.where((source == giver) & (target == own), key, NONE))
    for rank in range(CAPG):
        for place in range(len(OFFSETS)):
            at = place * CAPG + rank
            least = jnp.min(leaving[place])
            leaving[place] = jnp.where(leaving[place] > least, leaving[place], NONE)
            code = jnp.where(least < NONE, least, 0.0).astype(jnp.int32)
            fragment = (code >> 6) & 63
            meta_ref[at] = fragment
            sent_ref[at] = weight_ref[code >> 12, fragment]
            least = jnp.min(arriving[place])
            arriving[place] = jnp.where(arriving[place] > least, arriving[place], NONE)
            code = jnp.where(least < NONE, least, -1.0).astype(jnp.int32)
            meta_ref[SLOTS + at] = jnp.where(code >= 0, code & 63, -1)

    def invert(step, carry):
        meta_ref[2 * SLOTS + (partner_ref[step] & 63)] = step
        return carry

    lax.fori_loop(0, 64, invert, 0)
    middle = mid_ref[...]
    half = lax.broadcasted_iota(jnp.int32, middle.shape, 1) >> 6
    middle = jnp.where(half == own % 2, middle - own * 64, -1)
    coupling = jnp.concatenate([coupling_ref[...], coupling_ref[...]], axis=1)
    row = lax.broadcasted_iota(jnp.int32, (64, 128), 0)
    wide = jnp.zeros((64, 128), F32)
    for k in range(NN):
        wide = wide + jnp.where(middle[k : k + 1] == row, coupling[k : k + 1], 0.0)
    weights = wide[:, :64] + wide[:, 64:]
    first = weights.astype(BF16)
    rest = weights - first.astype(F32)
    second = rest.astype(BF16)
    local_ref[:, 0:64] = first
    local_ref[:, 64:128] = second
    local_ref[:, 128:192] = (rest - second.astype(F32)).astype(BF16)


def make_index(own, contacts, coupling, partner):
    def block(shift):
        return pl.BlockSpec((NN, 128), lambda i, s: (0, jnp.clip(s[0] // 2 + shift, 0, 31)))

    return pl.pallas_call(
        index_kernel,
        grid_spec=pltpu.PrefetchScalarGridSpec(
            num_scalar_prefetch=1,
            grid=(1,),
            in_specs=[block(-1), block(0), block(1), pl.BlockSpec((NN, 64), lambda i, s: (0, 0)), SMEM, SMEM],
            out_specs=[SMEM, SMEM, pl.BlockSpec((64, 192), lambda i, s: (0, 0))],
        ),
        out_shape=[
            jax.ShapeDtypeStruct((2 * SLOTS + 64,), jnp.int32),
            jax.ShapeDtypeStruct((SLOTS,), F32),
            jax.ShapeDtypeStruct((64, 192), BF16),
        ],
        name="slots",
    )(own, contacts, contacts, contacts, coupling, coupling, partner)


def assemble(whole, inner, own, other):
    whole[pl.ds(pl.multiple_of(inner * 128, 128), 128), :] = own
    whole[pl.ds(pl.multiple_of(128 - inner * 128, 128), 128), :] = other


def outgoing_kernel(meta_ref, inner_ref, sent_ref, *refs):
    count = len(OFFSETS)
    kernels, own, other, outs, whole = (
        refs[:count], refs[count : 2 * count], refs[2 * count : 3 * count], refs[3 * count : 4 * count], refs[-1]
    )
    step = pl.program_id(0)
    for place in range(count):
        assemble(whole.at[place], inner_ref[0], own[place][0], other[place][0])
        image = dot(kernels[place][0], whole[place]).astype(BF16)
        weight = sent_ref[place * CAPG + step]
        outs[place][0] = (image.astype(F32) * weight).astype(BF16)


def make_outgoing(meta, inner, sent, esp_kernel, density, other):
    count = len(OFFSETS)

    def block(place):
        return pl.BlockSpec((1, 128, 256), lambda c, m, i: (m[place * CAPG + c], 0, 0))

    blocks = [block(place) for place in range(count)]
    return pl.pallas_call(
        outgoing_kernel,
        grid_spec=pltpu.PrefetchScalarGridSpec(
            num_scalar_prefetch=2,
            grid=(CAPG,),
            in_specs=[SMEM] + blocks * 3,
            out_specs=[pl.BlockSpec((1, 128, 256), lambda c, m, i: (c, 0, 0))] * count,
            scratch_shapes=[pltpu.VMEM((count, 256, 256), BF16)],
        ),
        out_shape=[jax.ShapeDtypeStruct((CAPG, 128, 256), BF16)] * count,
        compiler_params=params(56),
        cost_estimate=SMALL,
        name="outgoing",
    )(meta, inner, sent, *[esp_kernel] * count, *[density] * count, *[other] * count)


def local_kernel(inner_ref, own, other, esp, response, core, weights, after, image_out, sum_out, part_out, wide, sums, whole):
    step = pl.program_id(0)
    loads = 64 // LOCAL_STEP

    @pl.when((step * LOCAL_STEP >= FIRST) & (step * LOCAL_STEP < FIRST + SECOND))
    def _():
        part_out[...] = own[...]

    @pl.when(step < loads)
    def _():
        for f in range(LOCAL_STEP):
            assemble(whole.at[f], inner_ref[0], own[f], other[f])
            both = jnp.concatenate([esp[f], response[f]], axis=0)
            result = dot(both, whole[f])
            image = result[:128].astype(BF16)
            image_out[f] = image
            rows = pl.ds(pl.multiple_of((step * LOCAL_STEP + f) * PITCH, 8), 128)
            image = image.astype(F32)
            total = result[128:] + core[f].astype(F32)
            for side in range(2):
                wide[side, rows, :] = image[:, side * 128 : side * 128 + 128]
                sums[side, rows, :] = total[:, side * 128 : side * 128 + 128]

    @pl.when(step >= loads)
    def _():
        matrix = weights[...]
        base = (step - loads) * ROW_STEP
        out = sum_out
        for r in range(ROW_STEP):
            at = pl.ds(base + r, 64, stride=PITCH)
            tile = jnp.concatenate([wide[0, at, :], wide[1, at, :]], axis=1).astype(BF16)
            mixed = dot(matrix, jnp.concatenate([tile, tile, tile], axis=0))
            for side in range(2):
                out[side, pl.ds(r, 64, stride=ROW_STEP), :] = (
                    mixed[:, side * 128 : side * 128 + 128] + sums[side, at, :]
                )


def make_local(inner, density, other, esp_kernel, coulomb_kernel, core_hamiltonian, weights, after):
    loads, rows = 64 // LOCAL_STEP, 128 // ROW_STEP
    block = pl.BlockSpec((LOCAL_STEP, 128, 256), lambda t, i: (jnp.minimum(t, loads - 1), 0, 0))
    return pl.pallas_call(
        local_kernel,
        grid_spec=pltpu.PrefetchScalarGridSpec(
            num_scalar_prefetch=1,
            grid=(loads + rows,),
            in_specs=[block] * 5 + [pl.BlockSpec((64, 192), lambda t, i: (0, 0)), ANY],
            out_specs=[
                block,
                pl.BlockSpec((2, 64 * ROW_STEP, 128), lambda t, i: (0, jnp.maximum(t - loads, 0), 0)),
                pl.BlockSpec(
                    (LOCAL_STEP, 128, 256),
                    lambda t, i: (jnp.clip(t - FIRST // LOCAL_STEP, 0, SECOND // LOCAL_STEP - 1), 0, 0),
                ),
            ],
            scratch_shapes=[
                pltpu.VMEM((2, 64 * PITCH, 128), F32),
                pltpu.VMEM((2, 64 * PITCH, 128), F32),
                pltpu.VMEM((LOCAL_STEP, 256, 256), BF16),
            ],
        ),
        out_shape=[
            jax.ShapeDtypeStruct((64, 128, 256), BF16),
            jax.ShapeDtypeStruct((2, rows * 64 * ROW_STEP, 128), F32),
            jax.ShapeDtypeStruct((SECOND, 128, 256), BF16),
        ],
        compiler_params=params(32),
        cost_estimate=SMALL,
        name="local",
    )(inner, density, other, esp_kernel, coulomb_kernel, core_hamiltonian, weights, after)


def fock_kernel(meta_ref, first_ref, began, sums, *refs):
    arrived, out, total = refs[:-2], refs[-2], refs[-1]
    step = pl.program_id(0)
    count = out.shape[0]
    for side in range(2):
        total[:, :, side * 128 : side * 128 + 128] = jnp.concatenate(
            [sums[side, tile].reshape(count, ROW_STEP, 128) for tile in range(128 // ROW_STEP)], axis=1
        )
    start = first_ref[0] + step * count
    for slot in range(SLOTS):
        place = meta_ref[SLOTS + slot] - start

        @pl.when((place >= 0) & (place < count))
        def _(slot=slot, place=place):
            total[place] += arrived[slot // CAPG][slot % CAPG].astype(F32)

    out[...] = total[...].astype(BF16)


def make_fock(meta, first, sums, arrived, began, number=32, count=8):
    tiles = 128 // ROW_STEP
    blocked = sums.reshape(2, tiles, 64 * ROW_STEP, 128)
    whole = pl.BlockSpec((CAPG, 128, 256), lambda t, m, f: (0, 0, 0))
    return pl.pallas_call(
        fock_kernel,
        grid_spec=pltpu.PrefetchScalarGridSpec(
            num_scalar_prefetch=2,
            grid=(number // count,),
            in_specs=[ANY, pl.BlockSpec((2, tiles, count * ROW_STEP, 128), lambda t, m, f: (0, 0, f[0] // count + t, 0))]
            + [whole] * len(OFFSETS),
            out_specs=pl.BlockSpec((count, 128, 256), lambda t, m, f: (t, 0, 0)),
            scratch_shapes=[pltpu.VMEM((count, 128, 256), F32)],
        ),
        out_shape=jax.ShapeDtypeStruct((number, 128, 256), BF16),
        compiler_params=params(48),
        cost_estimate=SMALL,
        name="fock_rows",
    )(meta, first, began, blocked, *arrived)


def pure_kernel(inner_ref, own, other, part, lines, fock_out, density_out, part_out, lines_out):
    part_out[...] = part[...]
    lines_out[...] = lines[...]
    row = lax.broadcasted_iota(jnp.int32, (256, 256), 0)
    column = lax.broadcasted_iota(jnp.int32, (256, 256), 1)
    diagonal = row == column
    identity = diagonal.astype(F32)
    turn = identity.astype(BF16)
    estimates = []
    for f in range(PURE_STEP):
        assemble(fock_out.at[f], inner_ref[0], own[f], other[f])
    for f in range(PURE_STEP):
        rows = fock_out[f]
        turned = lax.dot_general(turn, rows, (((1,), (1,)), ((), ())), preferred_element_type=F32)
        symmetric = 0.5 * (rows.astype(F32) + turned)
        centre = jnp.sum(jnp.where(diagonal, symmetric, 0.0), axis=(0, 1), keepdims=True) * (1.0 / 256)
        centred = symmetric - centre * identity
        spread = jnp.sqrt(jnp.sum(centred * centred, axis=(0, 1), keepdims=True) + 1e-6)
        estimates.append((0.5 * identity - centred * (0.5 / spread)).astype(BF16))
    for iteration in range(NPUR):
        squares = [dot(e, e).astype(BF16) for e in estimates]
        cubes = [dot(s, e) for s, e in zip(squares, estimates)]
        estimates = [(3.0 * s.astype(F32) - 2.0 * c).astype(BF16) for s, c in zip(squares, cubes)]
    for f in range(PURE_STEP):
        density_out[f] = estimates[f]


def make_pure(inner, own, other, density, lines):
    number = own.shape[0]
    last = 64 - FIRST - SECOND
    part = last // (number // PURE_STEP)
    skip = (FIRST + SECOND) // part
    rows = pl.BlockSpec((PURE_STEP, 128, 256), lambda t, i: (t, 0, 0))
    flat = pl.BlockSpec((64, 128), lambda t, i: (0, 0))
    whole = pl.BlockSpec((PURE_STEP, 256, 256), lambda t, i: (t, 0, 0))
    return pl.pallas_call(
        pure_kernel,
        grid_spec=pltpu.PrefetchScalarGridSpec(
            num_scalar_prefetch=1,
            grid=(number // PURE_STEP,),
            in_specs=[rows, rows, pl.BlockSpec((part, 128, 256), lambda t, i: (skip + t, 0, 0)), flat],
            out_specs=[whole, whole, pl.BlockSpec((part, 128, 256), lambda t, i: (t, 0, 0)), flat],
        ),
        out_shape=[jax.ShapeDtypeStruct((number, 256, 256), BF16)] * 2
        + [jax.ShapeDtypeStruct((last, 128, 256), BF16), jax.ShapeDtypeStruct((64, 128), F32)],
        compiler_params=params(28),
        cost_estimate=SMALL,
        name="purify",
    )(inner, own, other, density, lines)


def energy_kernel(meta_ref, first, swapped, before, *refs):
    images, out = refs[:-1], refs[-1]
    step = pl.program_id(0)

    @pl.when(step == 0)
    def _():
        out[...] = before[...]

    for f in range(ENERGY_STEP):
        product = swapped[f].astype(F32) * images[f][0].astype(F32)
        line = jnp.sum(product, axis=0, keepdims=True)
        place = meta_ref[2 * SLOTS + first + step * ENERGY_STEP + f]
        out[pl.ds(place, 1), :] = line[:, :128] + line[:, 128:]


def make_energy(meta, first, swapped, image, before):
    number = swapped.shape[0]

    def block(f):
        return pl.BlockSpec((1, 128, 256), lambda t, m: (m[2 * SLOTS + first + t * ENERGY_STEP + f], 0, 0))

    return pl.pallas_call(
        lambda meta_ref, *refs: energy_kernel(meta_ref, first, *refs),
        grid_spec=pltpu.PrefetchScalarGridSpec(
            num_scalar_prefetch=1,
            grid=(number // ENERGY_STEP,),
            in_specs=[
                pl.BlockSpec((ENERGY_STEP, 128, 256), lambda t, m: (t, 0, 0)),
                pl.BlockSpec((64, 128), lambda t, m: (0, 0)),
            ]
            + [block(f) for f in range(ENERGY_STEP)],
            out_specs=pl.BlockSpec((64, 128), lambda t, m: (0, 0)),
        ),
        out_shape=jax.ShapeDtypeStruct((64, 128), F32),
        cost_estimate=SMALL,
        name="energy",
    )(meta, swapped, before, *[image] * ENERGY_STEP)


def along(array, axis, by):
    length = lax.axis_size(axis)
    return lax.ppermute(array, axis, [(i, i + by) for i in range(length) if 0 <= i + by < length])


def exchanged(array, axis):
    return lax.ppermute(array, axis, [(i, i ^ 1) for i in range(lax.axis_size(axis))])


def body(density, core_hamiltonian, coulomb_kernel, esp_kernel, contacts, coupling, partner):
    own = lax.axis_index("frag").astype(jnp.int32).reshape(1)
    inner = lax.axis_index("inner").astype(jnp.int32).reshape(1)
    first = exchanged(density[:FIRST], "frag")
    other = exchanged(density, "inner")
    meta, sent, weights = make_index(own, contacts.T, coupling.T, partner)
    outgoing = make_outgoing(meta, inner, sent, esp_kernel, density, other)
    arrived = [along(block, "frag", by) for block, by in zip(outgoing, OFFSETS)]
    image, sums, part = make_local(
        inner, density, other, esp_kernel, coulomb_kernel, core_hamiltonian, weights, outgoing[-1]
    )
    second = exchanged(part, "frag")
    leave = make_fock(meta, 32 - inner * 32, sums, arrived, first)
    stay = make_fock(meta, inner * 32, sums, arrived, first)
    came = exchanged(leave, "inner")
    lines = make_energy(meta, 0, first, image, jnp.zeros((64, 128), F32))
    fock, new_density, part, lines = make_pure(inner, stay, came, density, lines)
    third = exchanged(part, "frag")
    lines = make_energy(meta, FIRST, second, image, lines)
    lines = make_energy(meta, FIRST + SECOND, third, image, lines)
    energy = lax.psum(jnp.sum(lines, axis=1) * (1.0 / 256), "inner")
    return (fock, new_density, energy)


def solution(mesh):
    rows = P("frag", "inner", None)
    whole = P(("frag", "inner"), None, None)
    return jax.shard_map(
        body,
        mesh=mesh,
        in_specs=(rows, rows, rows, rows, P(), P("frag", None), P("frag")),
        out_specs=(whole, whole, P("frag")),
        check_vma=False,
    )
```

```python
import functools

import jax
import jax.numpy as jnp
from jax import lax
from jax.experimental import pallas as pl
from jax.experimental.pallas import tpu as pltpu
from jax.sharding import PartitionSpec as P

NN = 16
CAPG = 4
NPUR = 6
OFFSETS = (1, -1, 2, -2)
SLOTS = len(OFFSETS) * CAPG
LOCAL_STEP = 8
ROW_STEP = 8
PITCH = 136
PURE_STEP = 8
ENERGY_STEP = 8
FIRST = 24
SECOND = 32
SHARES = (3, 1)
ANY = pl.BlockSpec(memory_space=pl.ANY)
NONE = float(1 << 20)
SMEM = pl.BlockSpec(memory_space=pltpu.SMEM)
SMALL = pl.CostEstimate(flops=1 << 16, bytes_accessed=1 << 12, transcendentals=0)
F32 = jnp.float32
BF16 = jnp.bfloat16


def dot(left, right):
    return jnp.dot(left, right, preferred_element_type=F32)


def params(mib):
    return pltpu.CompilerParams(vmem_limit_bytes=mib << 20)


def index_kernel(own_ref, low_ref, mid_ref, high_ref, coupling_ref, weight_ref, partner_ref, meta_ref, sent_ref, local_ref):
    own = own_ref[0]
    lists = jnp.concatenate([low_ref[...], mid_ref[...], high_ref[...]], axis=1)
    slot = lax.broadcasted_iota(jnp.int32, lists.shape, 0)
    lane = lax.broadcasted_iota(jnp.int32, lists.shape, 1)
    source = (own // 2 - 1) * 2 + (lane >> 6)
    target = lists >> 6
    key = (((slot * 64 + (lane & 63)) << 6) + (lists & 63)).astype(F32)
    leaving, arriving = [], []
    for offset in OFFSETS:
        leaving.append(jnp.where((source == own) & (target == own + offset), key, NONE))
        giver = own - offset
        giver = jnp.where((giver >= 0) & (giver < 64), giver, -999)
        arriving.append(jnp.where((source == giver) & (target == own), key, NONE))
    for rank in range(CAPG):
        for place in range(len(OFFSETS)):
            at = place * CAPG + rank
            least = jnp.min(leaving[place])
            leaving[place] = jnp.where(leaving[place] > least, leaving[place], NONE)
            code = jnp.where(least < NONE, least, 0.0).astype(jnp.int32)
            fragment = (code >> 6) & 63
            meta_ref[at] = fragment
            sent_ref[at] = weight_ref[code >> 12, fragment]
            least = jnp.min(arriving[place])
            arriving[place] = jnp.where(arriving[place] > least, arriving[place], NONE)
            code = jnp.where(least < NONE, least, -1.0).astype(jnp.int32)
            meta_ref[SLOTS + at] = jnp.where(code >= 0, code & 63, -1)

    def invert(step, carry):
        meta_ref[2 * SLOTS + (partner_ref[step] & 63)] = step
        return carry

    lax.fori_loop(0, 64, invert, 0)
    middle = mid_ref[...]
    half = lax.broadcasted_iota(jnp.int32, middle.shape, 1) >> 6
    middle = jnp.where(half == own % 2, middle - own * 64, -1)
    coupling = jnp.concatenate([coupling_ref[...], coupling_ref[...]], axis=1)
    row = lax.broadcasted_iota(jnp.int32, (64, 128), 0)
    wide = jnp.zeros((64, 128), F32)
    for k in range(NN):
        wide = wide + jnp.where(middle[k : k + 1] == row, coupling[k : k + 1], 0.0)
    weights = wide[:, :64] + wide[:, 64:]
    first = weights.astype(BF16)
    rest = weights - first.astype(F32)
    second = rest.astype(BF16)
    local_ref[:, 0:64] = first
    local_ref[:, 64:128] = second
    local_ref[:, 128:192] = (rest - second.astype(F32)).astype(BF16)


def make_index(own, contacts, coupling, partner):
    def block(shift):
        return pl.BlockSpec((NN, 128), lambda i, s: (0, jnp.clip(s[0] // 2 + shift, 0, 31)))

    return pl.pallas_call(
        index_kernel,
        grid_spec=pltpu.PrefetchScalarGridSpec(
            num_scalar_prefetch=1,
            grid=(1,),
            in_specs=[block(-1), block(0), block(1), pl.BlockSpec((NN, 64), lambda i, s: (0, 0)), SMEM, SMEM],
            out_specs=[SMEM, SMEM, pl.BlockSpec((64, 192), lambda i, s: (0, 0))],
        ),
        out_shape=[
            jax.ShapeDtypeStruct((2 * SLOTS + 64,), jnp.int32),
            jax.ShapeDtypeStruct((SLOTS,), F32),
            jax.ShapeDtypeStruct((64, 192), BF16),
        ],
        name="slots",
    )(own, contacts, contacts, contacts, coupling, coupling, partner)


def assemble(whole, inner, own, other):
    whole[pl.ds(pl.multiple_of(inner * 128, 128), 128), :] = own
    whole[pl.ds(pl.multiple_of(128 - inner * 128, 128), 128), :] = other


def outgoing_kernel(meta_ref, inner_ref, sent_ref, *refs):
    count = len(OFFSETS)
    kernels, own, other, outs, whole = (
        refs[:count], refs[count : 2 * count], refs[2 * count : 3 * count], refs[3 * count : 4 * count], refs[-1]
    )
    step = pl.program_id(0)
    for place in range(count):
        assemble(whole.at[place], inner_ref[0], own[place][0], other[place][0])
        image = dot(kernels[place][0], whole[place]).astype(BF16)
        weight = sent_ref[place * CAPG + step]
        outs[place][0] = (image.astype(F32) * weight).astype(BF16)


def make_outgoing(meta, inner, sent, esp_kernel, density, other):
    count = len(OFFSETS)

    def block(place):
        return pl.BlockSpec((1, 128, 256), lambda c, m, i: (m[place * CAPG + c], 0, 0))

    blocks = [block(place) for place in range(count)]
    return pl.pallas_call(
        outgoing_kernel,
        grid_spec=pltpu.PrefetchScalarGridSpec(
            num_scalar_prefetch=2,
            grid=(CAPG,),
            in_specs=[SMEM] + blocks * 3,
            out_specs=[pl.BlockSpec((1, 128, 256), lambda c, m, i: (c, 0, 0))] * count,
            scratch_shapes=[pltpu.VMEM((count, 256, 256), BF16)],
        ),
        out_shape=[jax.ShapeDtypeStruct((CAPG, 128, 256), BF16)] * count,
        compiler_params=params(56),
        cost_estimate=SMALL,
        name="outgoing",
    )(meta, inner, sent, *[esp_kernel] * count, *[density] * count, *[other] * count)


def local_kernel(inner_ref, own, other, esp, response, core, weights, after, image_out, sum_out, part_out, wide, sums, whole):
    step = pl.program_id(0)
    loads = 64 // LOCAL_STEP

    @pl.when((step * LOCAL_STEP >= FIRST) & (step * LOCAL_STEP < FIRST + SECOND))
    def _():
        part_out[...] = own[...]

    @pl.when(step < loads)
    def _():
        for f in range(LOCAL_STEP):
            assemble(whole.at[f], inner_ref[0], own[f], other[f])
            both = jnp.concatenate([esp[f], response[f]], axis=0)
            result = dot(both, whole[f])
            image = result[:128].astype(BF16)
            image_out[f] = image
            rows = pl.ds(pl.multiple_of((step * LOCAL_STEP + f) * PITCH, 8), 128)
            image = image.astype(F32)
            total = result[128:] + core[f].astype(F32)
            for side in range(2):
                wide[side, rows, :] = image[:, side * 128 : side * 128 + 128]
                sums[side, rows, :] = total[:, side * 128 : side * 128 + 128]

    @pl.when(step >= loads)
    def _():
        matrix = weights[...]
        base = (step - loads) * ROW_STEP
        out = sum_out
        for r in range(ROW_STEP):
            at = pl.ds(base + r, 64, stride=PITCH)
            tile = jnp.concatenate([wide[0, at, :], wide[1, at, :]], axis=1).astype(BF16)
            mixed = dot(matrix, jnp.concatenate([tile, tile, tile], axis=0))
            for side in range(2):
                out[side, pl.ds(r, 64, stride=ROW_STEP), :] = (
                    mixed[:, side * 128 : side * 128 + 128] + sums[side, at, :]
                )


def make_local(inner, density, other, esp_kernel, coulomb_kernel, core_hamiltonian, weights, after):
    loads, rows = 64 // LOCAL_STEP, 128 // ROW_STEP
    block = pl.BlockSpec((LOCAL_STEP, 128, 256), lambda t, i: (jnp.minimum(t, loads - 1), 0, 0))
    return pl.pallas_call(
        local_kernel,
        grid_spec=pltpu.PrefetchScalarGridSpec(
            num_scalar_prefetch=1,
            grid=(loads + rows,),
            in_specs=[block] * 5 + [pl.BlockSpec((64, 192), lambda t, i: (0, 0)), ANY],
            out_specs=[
                block,
                pl.BlockSpec((2, 64 * ROW_STEP, 128), lambda t, i: (0, jnp.maximum(t - loads, 0), 0)),
                pl.BlockSpec(
                    (LOCAL_STEP, 128, 256),
                    lambda t, i: (jnp.clip(t - FIRST // LOCAL_STEP, 0, SECOND // LOCAL_STEP - 1), 0, 0),
                ),
            ],
            scratch_shapes=[
                pltpu.VMEM((2, 64 * PITCH, 128), F32),
                pltpu.VMEM((2, 64 * PITCH, 128), F32),
                pltpu.VMEM((LOCAL_STEP, 256, 256), BF16),
            ],
        ),
        out_shape=[
            jax.ShapeDtypeStruct((64, 128, 256), BF16),
            jax.ShapeDtypeStruct((2, rows * 64 * ROW_STEP, 128), F32),
            jax.ShapeDtypeStruct((SECOND, 128, 256), BF16),
        ],
        compiler_params=params(32),
        cost_estimate=SMALL,
        name="local",
    )(inner, density, other, esp_kernel, coulomb_kernel, core_hamiltonian, weights, after)


def fock_kernel(shares, meta_ref, first_ref, began, sums, *refs):
    arrived, outs, total = refs[: len(OFFSETS)], refs[len(OFFSETS) : -1], refs[-1]
    step = pl.program_id(0)
    count = total.shape[0]
    for side in range(2):
        total[:, :, side * 128 : side * 128 + 128] = jnp.concatenate(
            [sums[side, tile].reshape(count, ROW_STEP, 128) for tile in range(128 // ROW_STEP)], axis=1
        )
    start = first_ref[0] + step * count
    for slot in range(SLOTS):
        place = meta_ref[SLOTS + slot] - start

        @pl.when((place >= 0) & (place < count))
        def _(slot=slot, place=place):
            total[place] += arrived[slot // CAPG][slot % CAPG].astype(F32)

    for part, out in enumerate(outs):
        low = sum(shares[:part])

        @pl.when((step >= low) & (step < low + shares[part]))
        def _(out=out):
            out[...] = total[...].astype(BF16)


def make_fock(meta, first, sums, arrived, began, shares, count=8):
    def out_block(part):
        low, steps = sum(shares[:part]), shares[part]
        return pl.BlockSpec((count, 128, 256), lambda t, m, f: (jnp.clip(t - low, 0, steps - 1), 0, 0))

    tiles = 128 // ROW_STEP
    blocked = sums.reshape(2, tiles, 64 * ROW_STEP, 128)
    whole = pl.BlockSpec((CAPG, 128, 256), lambda t, m, f: (0, 0, 0))
    return pl.pallas_call(
        functools.partial(fock_kernel, shares),
        grid_spec=pltpu.PrefetchScalarGridSpec(
            num_scalar_prefetch=2,
            grid=(sum(shares),),
            in_specs=[ANY, pl.BlockSpec((2, tiles, count * ROW_STEP, 128), lambda t, m, f: (0, 0, f[0] // count + t, 0))]
            + [whole] * len(OFFSETS),
            out_specs=[out_block(part) for part in range(len(shares))],
            scratch_shapes=[pltpu.VMEM((count, 128, 256), F32)],
        ),
        out_shape=[jax.ShapeDtypeStruct((share * count, 128, 256), BF16) for share in shares],
        compiler_params=params(48),
        cost_estimate=SMALL,
        name="fock_rows",
    )(meta, first, began, blocked, *arrived)


def pure_kernel(inner_ref, own, low, high, part, lines, fock_out, density_out, part_out, lines_out):
    early = pl.program_id(0) < SHARES[0]
    part_out[...] = part[...]
    lines_out[...] = lines[...]
    row = lax.broadcasted_iota(jnp.int32, (256, 256), 0)
    column = lax.broadcasted_iota(jnp.int32, (256, 256), 1)
    diagonal = row == column
    identity = diagonal.astype(F32)
    turn = identity.astype(BF16)
    estimates = []
    for f in range(PURE_STEP):
        assemble(fock_out.at[f], inner_ref[0], own[f], jnp.where(early, low[f], high[f]))
    for f in range(PURE_STEP):
        rows = fock_out[f]
        turned = lax.dot_general(turn, rows, (((1,), (1,)), ((), ())), preferred_element_type=F32)
        symmetric = 0.5 * (rows.astype(F32) + turned)
        centre = jnp.sum(jnp.where(diagonal, symmetric, 0.0), axis=(0, 1), keepdims=True) * (1.0 / 256)
        centred = symmetric - centre * identity
        spread = jnp.sqrt(jnp.sum(centred * centred, axis=(0, 1), keepdims=True) + 1e-6)
        estimates.append((0.5 * identity - centred * (0.5 / spread)).astype(BF16))
    for iteration in range(NPUR):
        squares = [dot(e, e).astype(BF16) for e in estimates]
        cubes = [dot(s, e) for s, e in zip(squares, estimates)]
        estimates = [(3.0 * s.astype(F32) - 2.0 * c).astype(BF16) for s, c in zip(squares, cubes)]
    for f in range(PURE_STEP):
        density_out[f] = estimates[f]


def make_pure(inner, own, low, high, density, lines):
    number = own.shape[0]
    last = 64 - FIRST - SECOND
    part = last // (number // PURE_STEP)
    skip = (FIRST + SECOND) // part
    rows = pl.BlockSpec((PURE_STEP, 128, 256), lambda t, i: (t, 0, 0))
    flat = pl.BlockSpec((64, 128), lambda t, i: (0, 0))
    half = SHARES[0]
    low_rows = pl.BlockSpec((PURE_STEP, 128, 256), lambda t, i: (jnp.minimum(t, half - 1), 0, 0))
    high_rows = pl.BlockSpec((PURE_STEP, 128, 256), lambda t, i: (jnp.maximum(t - half, 0), 0, 0))
    whole = pl.BlockSpec((PURE_STEP, 256, 256), lambda t, i: (t, 0, 0))
    return pl.pallas_call(
        pure_kernel,
        grid_spec=pltpu.PrefetchScalarGridSpec(
            num_scalar_prefetch=1,
            grid=(number // PURE_STEP,),
            in_specs=[rows, low_rows, high_rows, pl.BlockSpec((part, 128, 256), lambda t, i: (skip + t, 0, 0)), flat],
            out_specs=[whole, whole, pl.BlockSpec((part, 128, 256), lambda t, i: (t, 0, 0)), flat],
        ),
        out_shape=[jax.ShapeDtypeStruct((number, 256, 256), BF16)] * 2
        + [jax.ShapeDtypeStruct((last, 128, 256), BF16), jax.ShapeDtypeStruct((64, 128), F32)],
        compiler_params=params(28),
        cost_estimate=SMALL,
        name="purify",
    )(inner, own, low, high, density, lines)


def energy_kernel(meta_ref, first, swapped, before, *refs):
    images, out = refs[:-1], refs[-1]
    step = pl.program_id(0)

    @pl.when(step == 0)
    def _():
        out[...] = before[...]

    for f in range(ENERGY_STEP):
        product = swapped[f].astype(F32) * images[f][0].astype(F32)
        line = jnp.sum(product, axis=0, keepdims=True)
        place = meta_ref[2 * SLOTS + first + step * ENERGY_STEP + f]
        out[pl.ds(place, 1), :] = line[:, :128] + line[:, 128:]


def make_energy(meta, first, swapped, image, before):
    number = swapped.shape[0]

    def block(f):
        return pl.BlockSpec((1, 128, 256), lambda t, m: (m[2 * SLOTS + first + t * ENERGY_STEP + f], 0, 0))

    return pl.pallas_call(
        lambda meta_ref, *refs: energy_kernel(meta_ref, first, *refs),
        grid_spec=pltpu.PrefetchScalarGridSpec(
            num_scalar_prefetch=1,
            grid=(number // ENERGY_STEP,),
            in_specs=[
                pl.BlockSpec((ENERGY_STEP, 128, 256), lambda t, m: (t, 0, 0)),
                pl.BlockSpec((64, 128), lambda t, m: (0, 0)),
            ]
            + [block(f) for f in range(ENERGY_STEP)],
            out_specs=pl.BlockSpec((64, 128), lambda t, m: (0, 0)),
        ),
        out_shape=jax.ShapeDtypeStruct((64, 128), F32),
        cost_estimate=SMALL,
        name="energy",
    )(meta, swapped, before, *[image] * ENERGY_STEP)


def picked_kernel(meta_ref, *refs):
    for f, image in enumerate(refs[:-1]):
        refs[-1][f] = image[0]


def make_picked(meta, first, number, image):
    def block(f):
        return pl.BlockSpec((1, 128, 256), lambda t, m: (m[2 * SLOTS + first + f], 0, 0))

    return pl.pallas_call(
        picked_kernel,
        grid_spec=pltpu.PrefetchScalarGridSpec(
            num_scalar_prefetch=1,
            grid=(1,),
            in_specs=[block(f) for f in range(number)],
            out_specs=pl.BlockSpec((number, 128, 256), lambda t, m: (0, 0, 0)),
        ),
        out_shape=jax.ShapeDtypeStruct((number, 128, 256), BF16),
        cost_estimate=SMALL,
        name="picked",
    )(meta, *[image] * number)


def last_energy_kernel(meta_ref, first, swapped, before, image, out, lines):
    lines[0:64] = before[...]
    lines[64:128] = jnp.zeros((64, 128), F32)
    for f in range(swapped.shape[0]):
        place = meta_ref[2 * SLOTS + first + f]
        line = jnp.sum(swapped[f].astype(F32) * image[f].astype(F32), axis=0, keepdims=True)
        lines[pl.ds(place, 1), :] = line[:, :128] + line[:, 128:]
    out[...] = jnp.sum(lines[...].T, axis=0, keepdims=True)[:, :64] * (1.0 / 256)


def make_last_energy(meta, first, swapped, image, before):
    vmem = pl.BlockSpec(memory_space=pltpu.VMEM)
    return pl.pallas_call(
        lambda meta_ref, *refs: last_energy_kernel(meta_ref, first, *refs),
        in_specs=[SMEM, vmem, vmem, vmem],
        out_specs=vmem,
        out_shape=jax.ShapeDtypeStruct((1, 64), F32),
        scratch_shapes=[pltpu.VMEM((128, 128), F32)],
        cost_estimate=SMALL,
        compiler_params=params(16),
        name="energies",
    )(meta, swapped, before, image)


def along(array, axis, by):
    length = lax.axis_size(axis)
    return lax.ppermute(array, axis, [(i, i + by) for i in range(length) if 0 <= i + by < length])


def exchanged(array, axis):
    return lax.ppermute(array, axis, [(i, i ^ 1) for i in range(lax.axis_size(axis))])


def body(density, core_hamiltonian, coulomb_kernel, esp_kernel, contacts, coupling, partner):
    own = lax.axis_index("frag").astype(jnp.int32).reshape(1)
    inner = lax.axis_index("inner").astype(jnp.int32).reshape(1)
    first = exchanged(density[:FIRST], "frag")
    other = exchanged(density, "inner")
    meta, sent, weights = make_index(own, contacts.T, coupling.T, partner)
    outgoing = make_outgoing(meta, inner, sent, esp_kernel, density, other)
    arrived = [along(block, "frag", by) for block, by in zip(outgoing, OFFSETS)]
    image, sums, part = make_local(
        inner, density, other, esp_kernel, coulomb_kernel, core_hamiltonian, weights, outgoing[-1]
    )
    second = exchanged(part, "frag")
    low, high = make_fock(meta, 32 - inner * 32, sums, arrived, first, SHARES)
    (stay,) = make_fock(meta, inner * 32, sums, arrived, first, (sum(SHARES),))
    low, high = exchanged(low, "inner"), exchanged(high, "inner")
    lines = make_energy(meta, 0, first, image, jnp.zeros((64, 128), F32))
    fock, new_density, part, lines = make_pure(inner, stay, low, high, density, lines)
    third = exchanged(part, "frag")
    lines = make_energy(meta, FIRST, second, image, lines)
    picked = make_picked(meta, FIRST + SECOND, third.shape[0], image)
    partial = make_last_energy(meta, FIRST + SECOND, third, picked, lines)
    energy = lax.psum(partial.reshape(64), "inner")
    return (fock, new_density, energy)


def solution(mesh):
    rows = P("frag", "inner", None)
    whole = P(("frag", "inner"), None, None)
    return jax.shard_map(
        body,
        mesh=mesh,
        in_specs=(rows, rows, rows, rows, P(), P("frag", None), P("frag")),
        out_specs=(whole, whole, P("frag")),
        check_vma=False,
    )
```

```python
import functools

import jax
import jax.numpy as jnp
from jax import lax
from jax.experimental import pallas as pl
from jax.experimental.pallas import tpu as pltpu
from jax.sharding import PartitionSpec as P

NN = 16
CAPG = 4
NPUR = 6
OFFSETS = (1, -1, 2, -2)
SLOTS = len(OFFSETS) * CAPG
LOCAL_STEP = 8
ROW_STEP = 8
PITCH = 136
PURE_STEP = 8
ENERGY_STEP = 8
FIRST = 24
SECOND = 32
SHARES = (3, 1)
ANY = pl.BlockSpec(memory_space=pl.ANY)
NONE = float(1 << 20)
SMEM = pl.BlockSpec(memory_space=pltpu.SMEM)
SMALL = pl.CostEstimate(flops=1 << 16, bytes_accessed=1 << 12, transcendentals=0)
F32 = jnp.float32
BF16 = jnp.bfloat16


def dot(left, right):
    return jnp.dot(left, right, preferred_element_type=F32)


def params(mib):
    return pltpu.CompilerParams(vmem_limit_bytes=mib << 20)


def index_kernel(own_ref, low_ref, mid_ref, high_ref, coupling_ref, weight_ref, partner_ref, meta_ref, sent_ref, local_ref):
    own = own_ref[0]
    lists = jnp.concatenate([low_ref[...], mid_ref[...], high_ref[...]], axis=1)
    slot = lax.broadcasted_iota(jnp.int32, lists.shape, 0)
    lane = lax.broadcasted_iota(jnp.int32, lists.shape, 1)
    source = (own // 2 - 1) * 2 + (lane >> 6)
    target = lists >> 6
    key = (((slot * 64 + (lane & 63)) << 6) + (lists & 63)).astype(F32)
    leaving, arriving = [], []
    for offset in OFFSETS:
        leaving.append(jnp.where((source == own) & (target == own + offset), key, NONE))
        giver = own - offset
        giver = jnp.where((giver >= 0) & (giver < 64), giver, -999)
        arriving.append(jnp.where((source == giver) & (target == own), key, NONE))
    for rank in range(CAPG):
        for place in range(len(OFFSETS)):
            at = place * CAPG + rank
            least = jnp.min(leaving[place])
            leaving[place] = jnp.where(leaving[place] > least, leaving[place], NONE)
            code = jnp.where(least < NONE, least, 0.0).astype(jnp.int32)
            fragment = (code >> 6) & 63
            meta_ref[at] = fragment
            sent_ref[at] = weight_ref[code >> 12, fragment]
            least = jnp.min(arriving[place])
            arriving[place] = jnp.where(arriving[place] > least, arriving[place], NONE)
            code = jnp.where(least < NONE, least, -1.0).astype(jnp.int32)
            meta_ref[SLOTS + at] = jnp.where(code >= 0, code & 63, -1)

    def invert(step, carry):
        meta_ref[2 * SLOTS + (partner_ref[step] & 63)] = step
        return carry

    lax.fori_loop(0, 64, invert, 0)
    middle = mid_ref[...]
    half = lax.broadcasted_iota(jnp.int32, middle.shape, 1) >> 6
    middle = jnp.where(half == own % 2, middle - own * 64, -1)
    coupling = jnp.concatenate([coupling_ref[...], coupling_ref[...]], axis=1)
    row = lax.broadcasted_iota(jnp.int32, (64, 128), 0)
    wide = jnp.zeros((64, 128), F32)
    for k in range(NN):
        wide = wide + jnp.where(middle[k : k + 1] == row, coupling[k : k + 1], 0.0)
    weights = wide[:, :64] + wide[:, 64:]
    first = weights.astype(BF16)
    rest = weights - first.astype(F32)
    second = rest.astype(BF16)
    local_ref[:, 0:64] = first
    local_ref[:, 64:128] = second
    local_ref[:, 128:192] = (rest - second.astype(F32)).astype(BF16)


def make_index(own, contacts, coupling, partner):
    def block(shift):
        return pl.BlockSpec((NN, 128), lambda i, s: (0, jnp.clip(s[0] // 2 + shift, 0, 31)))

    return pl.pallas_call(
        index_kernel,
        grid_spec=pltpu.PrefetchScalarGridSpec(
            num_scalar_prefetch=1,
            grid=(1,),
            in_specs=[block(-1), block(0), block(1), pl.BlockSpec((NN, 64), lambda i, s: (0, 0)), SMEM, SMEM],
            out_specs=[SMEM, SMEM, pl.BlockSpec((64, 192), lambda i, s: (0, 0))],
        ),
        out_shape=[
            jax.ShapeDtypeStruct((2 * SLOTS + 64,), jnp.int32),
            jax.ShapeDtypeStruct((SLOTS,), F32),
            jax.ShapeDtypeStruct((64, 192), BF16),
        ],
        name="slots",
    )(own, contacts, contacts, contacts, coupling, coupling, partner)


def assemble(whole, inner, own, other):
    whole[pl.ds(pl.multiple_of(inner * 128, 128), 128), :] = own
    whole[pl.ds(pl.multiple_of(128 - inner * 128, 128), 128), :] = other


def outgoing_kernel(meta_ref, inner_ref, sent_ref, *refs):
    count = len(OFFSETS)
    kernels, own, other, outs, whole = (
        refs[:count], refs[count : 2 * count], refs[2 * count : 3 * count], refs[3 * count : 4 * count], refs[-1]
    )
    step = pl.program_id(0)
    for place in range(count):
        assemble(whole.at[place], inner_ref[0], own[place][0], other[place][0])
        image = dot(kernels[place][0], whole[place]).astype(BF16)
        weight = sent_ref[place * CAPG + step]
        outs[place][0] = (image.astype(F32) * weight).astype(BF16)


def make_outgoing(meta, inner, sent, esp_kernel, density, other):
    count = len(OFFSETS)

    def block(place):
        return pl.BlockSpec((1, 128, 256), lambda c, m, i: (m[place * CAPG + c], 0, 0))

    blocks = [block(place) for place in range(count)]
    return pl.pallas_call(
        outgoing_kernel,
        grid_spec=pltpu.PrefetchScalarGridSpec(
            num_scalar_prefetch=2,
            grid=(CAPG,),
            in_specs=[SMEM] + blocks * 3,
            out_specs=[pl.BlockSpec((1, 128, 256), lambda c, m, i: (c, 0, 0))] * count,
            scratch_shapes=[pltpu.VMEM((count, 256, 256), BF16)],
        ),
        out_shape=[jax.ShapeDtypeStruct((CAPG, 128, 256), BF16)] * count,
        compiler_params=params(56),
        cost_estimate=SMALL,
        name="outgoing",
    )(meta, inner, sent, *[esp_kernel] * count, *[density] * count, *[other] * count)


def local_kernel(inner_ref, own, other, esp, response, core, weights, after, image_out, sum_out, part_out, wide, sums, whole):
    step = pl.program_id(0)
    loads = 64 // LOCAL_STEP

    @pl.when((step * LOCAL_STEP >= FIRST) & (step * LOCAL_STEP < FIRST + SECOND))
    def _():
        part_out[...] = own[...]

    @pl.when(step < loads)
    def _():
        for f in range(LOCAL_STEP):
            assemble(whole.at[f], inner_ref[0], own[f], other[f])
            both = jnp.concatenate([esp[f], response[f]], axis=0)
            result = dot(both, whole[f])
            image = result[:128].astype(BF16)
            image_out[f] = image
            rows = pl.ds(pl.multiple_of((step * LOCAL_STEP + f) * PITCH, 8), 128)
            image = image.astype(F32)
            total = result[128:] + core[f].astype(F32)
            for side in range(2):
                wide[side, rows, :] = image[:, side * 128 : side * 128 + 128]
                sums[side, rows, :] = total[:, side * 128 : side * 128 + 128]

    @pl.when(step >= loads)
    def _():
        matrix = weights[...]
        base = (step - loads) * ROW_STEP
        out = sum_out
        for r in range(ROW_STEP):
            at = pl.ds(base + r, 64, stride=PITCH)
            tile = jnp.concatenate([wide[0, at, :], wide[1, at, :]], axis=1).astype(BF16)
            mixed = dot(matrix, jnp.concatenate([tile, tile, tile], axis=0))
            for side in range(2):
                out[side, pl.ds(r, 64, stride=ROW_STEP), :] = (
                    mixed[:, side * 128 : side * 128 + 128] + sums[side, at, :]
                )


def make_local(inner, density, other, esp_kernel, coulomb_kernel, core_hamiltonian, weights, after):
    loads, rows = 64 // LOCAL_STEP, 128 // ROW_STEP
    block = pl.BlockSpec((LOCAL_STEP, 128, 256), lambda t, i: (jnp.minimum(t, loads - 1), 0, 0))
    return pl.pallas_call(
        local_kernel,
        grid_spec=pltpu.PrefetchScalarGridSpec(
            num_scalar_prefetch=1,
            grid=(loads + rows,),
            in_specs=[block] * 5 + [pl.BlockSpec((64, 192), lambda t, i: (0, 0)), ANY],
            out_specs=[
                block,
                pl.BlockSpec((2, 64 * ROW_STEP, 128), lambda t, i: (0, jnp.maximum(t - loads, 0), 0)),
                pl.BlockSpec(
                    (LOCAL_STEP, 128, 256),
                    lambda t, i: (jnp.clip(t - FIRST // LOCAL_STEP, 0, SECOND // LOCAL_STEP - 1), 0, 0),
                ),
            ],
            scratch_shapes=[
                pltpu.VMEM((2, 64 * PITCH, 128), F32),
                pltpu.VMEM((2, 64 * PITCH, 128), F32),
                pltpu.VMEM((LOCAL_STEP, 256, 256), BF16),
            ],
        ),
        out_shape=[
            jax.ShapeDtypeStruct((64, 128, 256), BF16),
            jax.ShapeDtypeStruct((2, rows * 64 * ROW_STEP, 128), F32),
            jax.ShapeDtypeStruct((SECOND, 128, 256), BF16),
        ],
        compiler_params=params(32),
        cost_estimate=SMALL,
        name="local",
    )(inner, density, other, esp_kernel, coulomb_kernel, core_hamiltonian, weights, after)


def fock_kernel(shares, meta_ref, first_ref, lines, sums, *refs):
    arrived, outs, total = refs[: len(OFFSETS)], refs[len(OFFSETS) : -1], refs[-1]
    step = pl.program_id(0)
    count = total.shape[0]
    for side in range(2):
        total[:, :, side * 128 : side * 128 + 128] = jnp.concatenate(
            [sums[side, tile].reshape(count, ROW_STEP, 128) for tile in range(128 // ROW_STEP)], axis=1
        )
    start = first_ref[0] + step * count
    for slot in range(SLOTS):
        place = meta_ref[SLOTS + slot] - start

        @pl.when((place >= 0) & (place < count))
        def _(slot=slot, place=place):
            total[place] += arrived[slot // CAPG][slot % CAPG].astype(F32)

    for part, out in enumerate(outs):
        low = sum(shares[:part])

        @pl.when((step >= low) & (step < low + shares[part]))
        def _(out=out):
            out[...] = total[...].astype(BF16)


def make_fock(meta, first, sums, arrived, lines, shares, count=8):
    def out_block(part):
        low, steps = sum(shares[:part]), shares[part]
        return pl.BlockSpec((count, 128, 256), lambda t, m, f: (jnp.clip(t - low, 0, steps - 1), 0, 0))

    tiles = 128 // ROW_STEP
    blocked = sums.reshape(2, tiles, 64 * ROW_STEP, 128)
    whole = pl.BlockSpec((CAPG, 128, 256), lambda t, m, f: (0, 0, 0))
    return pl.pallas_call(
        functools.partial(fock_kernel, shares),
        grid_spec=pltpu.PrefetchScalarGridSpec(
            num_scalar_prefetch=2,
            grid=(sum(shares),),
            in_specs=[ANY, pl.BlockSpec((2, tiles, count * ROW_STEP, 128), lambda t, m, f: (0, 0, f[0] // count + t, 0))]
            + [whole] * len(OFFSETS),
            out_specs=[out_block(part) for part in range(len(shares))],
            scratch_shapes=[pltpu.VMEM((count, 128, 256), F32)],
        ),
        out_shape=[jax.ShapeDtypeStruct((share * count, 128, 256), BF16) for share in shares],
        compiler_params=params(48),
        cost_estimate=SMALL,
        name="fock_rows",
    )(meta, first, lines, blocked, *arrived)


def pure_kernel(inner_ref, own, low, high, part, lines, fock_out, density_out, part_out, lines_out):
    early = pl.program_id(0) < SHARES[0]
    part_out[...] = part[...]
    lines_out[...] = lines[...]
    row = lax.broadcasted_iota(jnp.int32, (256, 256), 0)
    column = lax.broadcasted_iota(jnp.int32, (256, 256), 1)
    diagonal = row == column
    identity = diagonal.astype(F32)
    turn = identity.astype(BF16)
    estimates = []
    for f in range(PURE_STEP):
        assemble(fock_out.at[f], inner_ref[0], own[f], jnp.where(early, low[f], high[f]))
    for f in range(PURE_STEP):
        rows = fock_out[f]
        turned = lax.dot_general(turn, rows, (((1,), (1,)), ((), ())), preferred_element_type=F32)
        symmetric = 0.5 * (rows.astype(F32) + turned)
        centre = jnp.sum(jnp.where(diagonal, symmetric, 0.0), axis=(0, 1), keepdims=True) * (1.0 / 256)
        centred = symmetric - centre * identity
        spread = jnp.sqrt(jnp.sum(centred * centred, axis=(0, 1), keepdims=True) + 1e-6)
        estimates.append((0.5 * identity - centred * (0.5 / spread)).astype(BF16))
    for iteration in range(NPUR):
        squares = [dot(e, e).astype(BF16) for e in estimates]
        cubes = [dot(s, e) for s, e in zip(squares, estimates)]
        estimates = [(3.0 * s.astype(F32) - 2.0 * c).astype(BF16) for s, c in zip(squares, cubes)]
    for f in range(PURE_STEP):
        density_out[f] = estimates[f]


def make_pure(inner, own, low, high, density, lines):
    number = own.shape[0]
    last = 64 - FIRST - SECOND
    part = last // (number // PURE_STEP)
    skip = (FIRST + SECOND) // part
    rows = pl.BlockSpec((PURE_STEP, 128, 256), lambda t, i: (t, 0, 0))
    flat = pl.BlockSpec((64, 128), lambda t, i: (0, 0))
    half = SHARES[0]
    low_rows = pl.BlockSpec((PURE_STEP, 128, 256), lambda t, i: (jnp.minimum(t, half - 1), 0, 0))
    high_rows = pl.BlockSpec((PURE_STEP, 128, 256), lambda t, i: (jnp.maximum(t - half, 0), 0, 0))
    whole = pl.BlockSpec((PURE_STEP, 256, 256), lambda t, i: (t, 0, 0))
    return pl.pallas_call(
        pure_kernel,
        grid_spec=pltpu.PrefetchScalarGridSpec(
            num_scalar_prefetch=1,
            grid=(number // PURE_STEP,),
            in_specs=[rows, low_rows, high_rows, pl.BlockSpec((part, 128, 256), lambda t, i: (skip + t, 0, 0)), flat],
            out_specs=[whole, whole, pl.BlockSpec((part, 128, 256), lambda t, i: (t, 0, 0)), flat],
        ),
        out_shape=[jax.ShapeDtypeStruct((number, 256, 256), BF16)] * 2
        + [jax.ShapeDtypeStruct((last, 128, 256), BF16), jax.ShapeDtypeStruct((64, 128), F32)],
        compiler_params=params(28),
        cost_estimate=SMALL,
        name="purify",
    )(inner, own, low, high, density, lines)


def energy_kernel(meta_ref, first, swapped, before, *refs):
    images, out = refs[:-1], refs[-1]
    step = pl.program_id(0)

    @pl.when(step == 0)
    def _():
        out[...] = before[...]

    for f in range(ENERGY_STEP):
        product = swapped[f].astype(F32) * images[f][0].astype(F32)
        line = jnp.sum(product, axis=0, keepdims=True)
        place = meta_ref[2 * SLOTS + first + step * ENERGY_STEP + f]
        out[pl.ds(place, 1), :] = line[:, :128] + line[:, 128:]


def make_energy(meta, first, swapped, image, before):
    number = swapped.shape[0]

    def block(f):
        return pl.BlockSpec((1, 128, 256), lambda t, m: (m[2 * SLOTS + first + t * ENERGY_STEP + f], 0, 0))

    return pl.pallas_call(
        lambda meta_ref, *refs: energy_kernel(meta_ref, first, *refs),
        grid_spec=pltpu.PrefetchScalarGridSpec(
            num_scalar_prefetch=1,
            grid=(number // ENERGY_STEP,),
            in_specs=[
                pl.BlockSpec((ENERGY_STEP, 128, 256), lambda t, m: (t, 0, 0)),
                pl.BlockSpec((64, 128), lambda t, m: (0, 0)),
            ]
            + [block(f) for f in range(ENERGY_STEP)],
            out_specs=pl.BlockSpec((64, 128), lambda t, m: (0, 0)),
        ),
        out_shape=jax.ShapeDtypeStruct((64, 128), F32),
        cost_estimate=SMALL,
        name="energy",
    )(meta, swapped, before, *[image] * ENERGY_STEP)


def picked_kernel(meta_ref, *refs):
    for f, image in enumerate(refs[:-1]):
        refs[-1][f] = image[0]


def make_picked(meta, first, number, image):
    def block(f):
        return pl.BlockSpec((1, 128, 256), lambda t, m: (m[2 * SLOTS + first + f], 0, 0))

    return pl.pallas_call(
        picked_kernel,
        grid_spec=pltpu.PrefetchScalarGridSpec(
            num_scalar_prefetch=1,
            grid=(1,),
            in_specs=[block(f) for f in range(number)],
            out_specs=pl.BlockSpec((number, 128, 256), lambda t, m: (0, 0, 0)),
        ),
        out_shape=jax.ShapeDtypeStruct((number, 128, 256), BF16),
        cost_estimate=SMALL,
        name="picked",
    )(meta, *[image] * number)


def last_energy_kernel(meta_ref, first, swapped, before, image, out, lines):
    lines[0:64] = before[...]
    lines[64:128] = jnp.zeros((64, 128), F32)
    for f in range(swapped.shape[0]):
        place = meta_ref[2 * SLOTS + first + f]
        line = jnp.sum(swapped[f].astype(F32) * image[f].astype(F32), axis=0, keepdims=True)
        lines[pl.ds(place, 1), :] = line[:, :128] + line[:, 128:]
    out[...] = jnp.sum(lines[...].T, axis=0, keepdims=True)[:, :64] * (1.0 / 256)


def make_last_energy(meta, first, swapped, image, before):
    vmem = pl.BlockSpec(memory_space=pltpu.VMEM)
    return pl.pallas_call(
        lambda meta_ref, *refs: last_energy_kernel(meta_ref, first, *refs),
        in_specs=[SMEM, vmem, vmem, vmem],
        out_specs=vmem,
        out_shape=jax.ShapeDtypeStruct((1, 64), F32),
        scratch_shapes=[pltpu.VMEM((128, 128), F32)],
        cost_estimate=SMALL,
        compiler_params=params(16),
        name="energies",
    )(meta, swapped, before, image)


def taken_kernel(whole, out, done):
    copies = []
    for part in range(4):
        rows = pl.ds(part * (FIRST // 4), FIRST // 4)
        copies.append(pltpu.make_async_copy(whole.at[rows], out.at[rows], done.at[part]))
        copies[-1].start()
    for copy in copies:
        copy.wait()


def make_taken(density):
    return pl.pallas_call(
        taken_kernel,
        in_specs=[ANY],
        out_specs=pl.BlockSpec(memory_space=pltpu.VMEM),
        out_shape=jax.ShapeDtypeStruct((FIRST, 128, 256), BF16),
        scratch_shapes=[pltpu.SemaphoreType.DMA((4,))],
        cost_estimate=SMALL,
        compiler_params=params(60),
        name="taken",
    )(density)


def along(array, axis, by):
    length = lax.axis_size(axis)
    return lax.ppermute(array, axis, [(i, i + by) for i in range(length) if 0 <= i + by < length])


def exchanged(array, axis):
    return lax.ppermute(array, axis, [(i, i ^ 1) for i in range(lax.axis_size(axis))])


def body(density, core_hamiltonian, coulomb_kernel, esp_kernel, contacts, coupling, partner):
    own = lax.axis_index("frag").astype(jnp.int32).reshape(1)
    inner = lax.axis_index("inner").astype(jnp.int32).reshape(1)
    first = exchanged(make_taken(density), "frag")
    other = exchanged(density, "inner")
    meta, sent, weights = make_index(own, contacts.T, coupling.T, partner)
    outgoing = make_outgoing(meta, inner, sent, esp_kernel, density, other)
    arrived = [along(block, "frag", by) for block, by in zip(outgoing, OFFSETS)]
    image, sums, part = make_local(
        inner, density, other, esp_kernel, coulomb_kernel, core_hamiltonian, weights, outgoing[-1]
    )
    second = exchanged(part, "frag")
    lines = make_energy(meta, 0, first, image, jnp.zeros((64, 128), F32))
    low, high = make_fock(meta, 32 - inner * 32, sums, arrived, lines, SHARES)
    (stay,) = make_fock(meta, inner * 32, sums, arrived, lines, (sum(SHARES),))
    low, high = exchanged(low, "inner"), exchanged(high, "inner")
    fock, new_density, part, lines = make_pure(inner, stay, low, high, density, lines)
    third = exchanged(part, "frag")
    picked = make_picked(meta, FIRST + SECOND, third.shape[0], image)
    lines = make_energy(meta, FIRST, second, image, lines)
    partial = make_last_energy(meta, FIRST + SECOND, third, picked, lines)
    energy = lax.psum(partial.reshape(64), "inner")
    return (fock, new_density, energy)


def solution(mesh):
    rows = P("frag", "inner", None)
    whole = P(("frag", "inner"), None, None)
    return jax.shard_map(
        body,
        mesh=mesh,
        in_specs=(rows, rows, rows, rows, P(), P("frag", None), P("frag")),
        out_specs=(whole, whole, P("frag")),
        check_vma=False,
    )
```

```python
import functools

import jax
import jax.numpy as jnp
from jax import lax
from jax.experimental import pallas as pl
from jax.experimental.pallas import tpu as pltpu
from jax.sharding import PartitionSpec as P

NN = 16
CAPG = 4
NPUR = 6
OFFSETS = (1, -1, 2, -2)
SLOTS = len(OFFSETS) * CAPG
LOCAL_STEP = 8
ROW_STEP = 8
PITCH = 136
PURE_STEP = 8
ENERGY_STEP = 8
FIRST = 24
SECOND = 32
SHARES = (3, 1)
ANY = pl.BlockSpec(memory_space=pl.ANY)
NONE = float(1 << 20)
SMEM = pl.BlockSpec(memory_space=pltpu.SMEM)
SMALL = pl.CostEstimate(flops=1 << 16, bytes_accessed=1 << 12, transcendentals=0)
F32 = jnp.float32
BF16 = jnp.bfloat16


def dot(left, right):
    return jnp.dot(left, right, preferred_element_type=F32)


def params(mib):
    return pltpu.CompilerParams(vmem_limit_bytes=mib << 20)


def index_kernel(own_ref, low_ref, mid_ref, high_ref, coupling_ref, weight_ref, partner_ref, meta_ref, sent_ref, local_ref):
    own = own_ref[0]
    lists = jnp.concatenate([low_ref[...], mid_ref[...], high_ref[...]], axis=1)
    slot = lax.broadcasted_iota(jnp.int32, lists.shape, 0)
    lane = lax.broadcasted_iota(jnp.int32, lists.shape, 1)
    source = (own // 2 - 1) * 2 + (lane >> 6)
    target = lists >> 6
    key = (((slot * 64 + (lane & 63)) << 6) + (lists & 63)).astype(F32)
    leaving, arriving = [], []
    for offset in OFFSETS:
        leaving.append(jnp.where((source == own) & (target == own + offset), key, NONE))
        giver = own - offset
        giver = jnp.where((giver >= 0) & (giver < 64), giver, -999)
        arriving.append(jnp.where((source == giver) & (target == own), key, NONE))
    for rank in range(CAPG):
        for place in range(len(OFFSETS)):
            at = place * CAPG + rank
            least = jnp.min(leaving[place])
            leaving[place] = jnp.where(leaving[place] > least, leaving[place], NONE)
            code = jnp.where(least < NONE, least, 0.0).astype(jnp.int32)
            fragment = (code >> 6) & 63
            meta_ref[at] = fragment
            sent_ref[at] = weight_ref[code >> 12, fragment]
            least = jnp.min(arriving[place])
            arriving[place] = jnp.where(arriving[place] > least, arriving[place], NONE)
            code = jnp.where(least < NONE, least, -1.0).astype(jnp.int32)
            meta_ref[SLOTS + at] = jnp.where(code >= 0, code & 63, -1)

    def invert(step, carry):
        meta_ref[2 * SLOTS + (partner_ref[step] & 63)] = step
        return carry

    lax.fori_loop(0, 64, invert, 0)
    middle = mid_ref[...]
    half = lax.broadcasted_iota(jnp.int32, middle.shape, 1) >> 6
    middle = jnp.where(half == own % 2, middle - own * 64, -1)
    coupling = jnp.concatenate([coupling_ref[...], coupling_ref[...]], axis=1)
    row = lax.broadcasted_iota(jnp.int32, (64, 128), 0)
    wide = jnp.zeros((64, 128), F32)
    for k in range(NN):
        wide = wide + jnp.where(middle[k : k + 1] == row, coupling[k : k + 1], 0.0)
    weights = wide[:, :64] + wide[:, 64:]
    first = weights.astype(BF16)
    rest = weights - first.astype(F32)
    second = rest.astype(BF16)
    local_ref[:, 0:64] = first
    local_ref[:, 64:128] = second
    local_ref[:, 128:192] = (rest - second.astype(F32)).astype(BF16)


def make_index(own, contacts, coupling, partner):
    def block(shift):
        return pl.BlockSpec((NN, 128), lambda i, s: (0, jnp.clip(s[0] // 2 + shift, 0, 31)))

    return pl.pallas_call(
        index_kernel,
        grid_spec=pltpu.PrefetchScalarGridSpec(
            num_scalar_prefetch=1,
            grid=(1,),
            in_specs=[block(-1), block(0), block(1), pl.BlockSpec((NN, 64), lambda i, s: (0, 0)), SMEM, SMEM],
            out_specs=[SMEM, SMEM, pl.BlockSpec((64, 192), lambda i, s: (0, 0))],
        ),
        out_shape=[
            jax.ShapeDtypeStruct((2 * SLOTS + 64,), jnp.int32),
            jax.ShapeDtypeStruct((SLOTS,), F32),
            jax.ShapeDtypeStruct((64, 192), BF16),
        ],
        name="slots",
    )(own, contacts, contacts, contacts, coupling, coupling, partner)


def assemble(whole, inner, own, other):
    whole[pl.ds(pl.multiple_of(inner * 128, 128), 128), :] = own
    whole[pl.ds(pl.multiple_of(128 - inner * 128, 128), 128), :] = other


def outgoing_kernel(meta_ref, inner_ref, sent_ref, *refs):
    count = len(OFFSETS)
    kernels, own, other, outs, whole = (
        refs[:count], refs[count : 2 * count], refs[2 * count : 3 * count], refs[3 * count : 4 * count], refs[-1]
    )
    step = pl.program_id(0)
    for place in range(count):
        assemble(whole.at[place], inner_ref[0], own[place][0], other[place][0])
        image = dot(kernels[place][0], whole[place]).astype(BF16)
        weight = sent_ref[place * CAPG + step]
        outs[place][0] = (image.astype(F32) * weight).astype(BF16)


def make_outgoing(meta, inner, sent, esp_kernel, density, other):
    count = len(OFFSETS)

    def block(place):
        return pl.BlockSpec((1, 128, 256), lambda c, m, i: (m[place * CAPG + c], 0, 0))

    blocks = [block(place) for place in range(count)]
    return pl.pallas_call(
        outgoing_kernel,
        grid_spec=pltpu.PrefetchScalarGridSpec(
            num_scalar_prefetch=2,
            grid=(CAPG,),
            in_specs=[SMEM] + blocks * 3,
            out_specs=[pl.BlockSpec((1, 128, 256), lambda c, m, i: (c, 0, 0))] * count,
            scratch_shapes=[pltpu.VMEM((count, 256, 256), BF16)],
        ),
        out_shape=[jax.ShapeDtypeStruct((CAPG, 128, 256), BF16)] * count,
        compiler_params=params(56),
        cost_estimate=SMALL,
        name="outgoing",
    )(meta, inner, sent, *[esp_kernel] * count, *[density] * count, *[other] * count)


def local_kernel(inner_ref, own, other, esp, response, core, weights, after, image_out, sum_out, part_out, wide, sums, whole):
    step = pl.program_id(0)
    loads = 64 // LOCAL_STEP

    @pl.when((step * LOCAL_STEP >= FIRST) & (step * LOCAL_STEP < FIRST + SECOND))
    def _():
        part_out[...] = own[...]

    @pl.when(step < loads)
    def _():
        for f in range(LOCAL_STEP):
            assemble(whole.at[f], inner_ref[0], own[f], other[f])
            both = jnp.concatenate([esp[f], response[f]], axis=0)
            result = dot(both, whole[f])
            image = result[:128].astype(BF16)
            image_out[f] = image
            rows = pl.ds(pl.multiple_of((step * LOCAL_STEP + f) * PITCH, 8), 128)
            image = image.astype(F32)
            total = result[128:] + core[f].astype(F32)
            for side in range(2):
                wide[side, rows, :] = image[:, side * 128 : side * 128 + 128]
                sums[side, rows, :] = total[:, side * 128 : side * 128 + 128]

    @pl.when(step >= loads)
    def _():
        matrix = weights[...]
        base = (step - loads) * ROW_STEP
        out = sum_out
        for r in range(ROW_STEP):
            at = pl.ds(base + r, 64, stride=PITCH)
            tile = jnp.concatenate([wide[0, at, :], wide[1, at, :]], axis=1).astype(BF16)
            mixed = dot(matrix, jnp.concatenate([tile, tile, tile], axis=0))
            for side in range(2):
                out[side, pl.ds(r, 64, stride=ROW_STEP), :] = (
                    mixed[:, side * 128 : side * 128 + 128] + sums[side, at, :]
                )


def make_local(inner, density, other, esp_kernel, coulomb_kernel, core_hamiltonian, weights, after):
    loads, rows = 64 // LOCAL_STEP, 128 // ROW_STEP
    block = pl.BlockSpec((LOCAL_STEP, 128, 256), lambda t, i: (jnp.minimum(t, loads - 1), 0, 0))
    return pl.pallas_call(
        local_kernel,
        grid_spec=pltpu.PrefetchScalarGridSpec(
            num_scalar_prefetch=1,
            grid=(loads + rows,),
            in_specs=[block] * 5 + [pl.BlockSpec((64, 192), lambda t, i: (0, 0)), ANY],
            out_specs=[
                block,
                pl.BlockSpec((2, 64 * ROW_STEP, 128), lambda t, i: (0, jnp.maximum(t - loads, 0), 0)),
                pl.BlockSpec(
                    (LOCAL_STEP, 128, 256),
                    lambda t, i: (jnp.clip(t - FIRST // LOCAL_STEP, 0, SECOND // LOCAL_STEP - 1), 0, 0),
                ),
            ],
            scratch_shapes=[
                pltpu.VMEM((2, 64 * PITCH, 128), F32),
                pltpu.VMEM((2, 64 * PITCH, 128), F32),
                pltpu.VMEM((LOCAL_STEP, 256, 256), BF16),
            ],
        ),
        out_shape=[
            jax.ShapeDtypeStruct((64, 128, 256), BF16),
            jax.ShapeDtypeStruct((2, rows * 64 * ROW_STEP, 128), F32),
            jax.ShapeDtypeStruct((SECOND, 128, 256), BF16),
        ],
        compiler_params=params(32),
        cost_estimate=SMALL,
        name="local",
    )(inner, density, other, esp_kernel, coulomb_kernel, core_hamiltonian, weights, after)


def fock_kernel(shares, meta_ref, first_ref, lines, sums, *refs):
    arrived, outs, total = refs[: len(OFFSETS)], refs[len(OFFSETS) : -1], refs[-1]
    step = pl.program_id(0)
    count = total.shape[0]
    for side in range(2):
        total[:, :, side * 128 : side * 128 + 128] = jnp.concatenate(
            [sums[side, tile].reshape(count, ROW_STEP, 128) for tile in range(128 // ROW_STEP)], axis=1
        )
    start = first_ref[0] + step * count
    for slot in range(SLOTS):
        place = meta_ref[SLOTS + slot] - start

        @pl.when((place >= 0) & (place < count))
        def _(slot=slot, place=place):
            total[place] += arrived[slot // CAPG][slot % CAPG].astype(F32)

    for part, out in enumerate(outs):
        low = sum(shares[:part])

        @pl.when((step >= low) & (step < low + shares[part]))
        def _(out=out):
            out[...] = total[...].astype(BF16)


def make_fock(meta, first, sums, arrived, lines, shares, count=8):
    def out_block(part):
        low, steps = sum(shares[:part]), shares[part]
        return pl.BlockSpec((count, 128, 256), lambda t, m, f: (jnp.clip(t - low, 0, steps - 1), 0, 0))

    tiles = 128 // ROW_STEP
    blocked = sums.reshape(2, tiles, 64 * ROW_STEP, 128)
    whole = pl.BlockSpec((CAPG, 128, 256), lambda t, m, f: (0, 0, 0))
    return pl.pallas_call(
        functools.partial(fock_kernel, shares),
        grid_spec=pltpu.PrefetchScalarGridSpec(
            num_scalar_prefetch=2,
            grid=(sum(shares),),
            in_specs=[ANY, pl.BlockSpec((2, tiles, count * ROW_STEP, 128), lambda t, m, f: (0, 0, f[0] // count + t, 0))]
            + [whole] * len(OFFSETS),
            out_specs=[out_block(part) for part in range(len(shares))],
            scratch_shapes=[pltpu.VMEM((count, 128, 256), F32)],
        ),
        out_shape=[jax.ShapeDtypeStruct((share * count, 128, 256), BF16) for share in shares],
        compiler_params=params(48),
        cost_estimate=SMALL,
        name="fock_rows",
    )(meta, first, lines, blocked, *arrived)


def pure_kernel(inner_ref, own, low, high, part, lines, fock_out, density_out, part_out, lines_out):
    early = pl.program_id(0) < SHARES[0]
    part_out[...] = part[...]
    lines_out[...] = lines[...]
    row = lax.broadcasted_iota(jnp.int32, (256, 256), 0)
    column = lax.broadcasted_iota(jnp.int32, (256, 256), 1)
    diagonal = row == column
    identity = diagonal.astype(F32)
    turn = identity.astype(BF16)
    estimates = []
    for f in range(PURE_STEP):
        assemble(fock_out.at[f], inner_ref[0], own[f], jnp.where(early, low[f], high[f]))
    for f in range(PURE_STEP):
        rows = fock_out[f]
        turned = lax.dot_general(turn, rows, (((1,), (1,)), ((), ())), preferred_element_type=F32)
        symmetric = 0.5 * (rows.astype(F32) + turned)
        centre = jnp.sum(jnp.where(diagonal, symmetric, 0.0), axis=(0, 1), keepdims=True) * (1.0 / 256)
        centred = symmetric - centre * identity
        spread = jnp.sqrt(jnp.sum(centred * centred, axis=(0, 1), keepdims=True) + 1e-6)
        estimates.append((0.5 * identity - centred * (0.5 / spread)).astype(BF16))
    for iteration in range(NPUR):
        squares = [dot(e, e).astype(BF16) for e in estimates]
        cubes = [dot(s, e) for s, e in zip(squares, estimates)]
        estimates = [(3.0 * s.astype(F32) - 2.0 * c).astype(BF16) for s, c in zip(squares, cubes)]
    for f in range(PURE_STEP):
        density_out[f] = estimates[f]


def make_pure(inner, own, low, high, density, lines):
    number = own.shape[0]
    last = 64 - FIRST - SECOND
    part = last // (number // PURE_STEP)
    skip = (FIRST + SECOND) // part
    rows = pl.BlockSpec((PURE_STEP, 128, 256), lambda t, i: (t, 0, 0))
    flat = pl.BlockSpec((64, 128), lambda t, i: (0, 0))
    half = SHARES[0]
    low_rows = pl.BlockSpec((PURE_STEP, 128, 256), lambda t, i: (jnp.minimum(t, half - 1), 0, 0))
    high_rows = pl.BlockSpec((PURE_STEP, 128, 256), lambda t, i: (jnp.maximum(t - half, 0), 0, 0))
    whole = pl.BlockSpec((PURE_STEP, 256, 256), lambda t, i: (t, 0, 0))
    return pl.pallas_call(
        pure_kernel,
        grid_spec=pltpu.PrefetchScalarGridSpec(
            num_scalar_prefetch=1,
            grid=(number // PURE_STEP,),
            in_specs=[rows, low_rows, high_rows, pl.BlockSpec((part, 128, 256), lambda t, i: (skip + t, 0, 0)), flat],
            out_specs=[whole, whole, pl.BlockSpec((part, 128, 256), lambda t, i: (t, 0, 0)), flat],
        ),
        out_shape=[jax.ShapeDtypeStruct((number, 256, 256), BF16)] * 2
        + [jax.ShapeDtypeStruct((last, 128, 256), BF16), jax.ShapeDtypeStruct((64, 128), F32)],
        compiler_params=params(28),
        cost_estimate=SMALL,
        name="purify",
    )(inner, own, low, high, density, lines)


def energy_kernel(meta_ref, first, swapped, before, *refs):
    images, out = refs[:-1], refs[-1]
    step = pl.program_id(0)

    @pl.when(step == 0)
    def _():
        out[...] = before[...]

    for f in range(ENERGY_STEP):
        product = swapped[f].astype(F32) * images[f][0].astype(F32)
        line = jnp.sum(product, axis=0, keepdims=True)
        place = meta_ref[2 * SLOTS + first + step * ENERGY_STEP + f]
        out[pl.ds(place, 1), :] = line[:, :128] + line[:, 128:]


def make_energy(meta, first, swapped, image, before):
    number = swapped.shape[0]

    def block(f):
        return pl.BlockSpec((1, 128, 256), lambda t, m: (m[2 * SLOTS + first + t * ENERGY_STEP + f], 0, 0))

    return pl.pallas_call(
        lambda meta_ref, *refs: energy_kernel(meta_ref, first, *refs),
        grid_spec=pltpu.PrefetchScalarGridSpec(
            num_scalar_prefetch=1,
            grid=(number // ENERGY_STEP,),
            in_specs=[
                pl.BlockSpec((ENERGY_STEP, 128, 256), lambda t, m: (t, 0, 0)),
                pl.BlockSpec((64, 128), lambda t, m: (0, 0)),
            ]
            + [block(f) for f in range(ENERGY_STEP)],
            out_specs=pl.BlockSpec((64, 128), lambda t, m: (0, 0)),
        ),
        out_shape=jax.ShapeDtypeStruct((64, 128), F32),
        cost_estimate=SMALL,
        compiler_params=params(20),
        name="energy",
    )(meta, swapped, before, *[image] * ENERGY_STEP)


def picked_kernel(meta_ref, *refs):
    for f, image in enumerate(refs[:-1]):
        refs[-1][f] = image[0]


def make_picked(meta, first, number, image):
    def block(f):
        return pl.BlockSpec((1, 128, 256), lambda t, m: (m[2 * SLOTS + first + f], 0, 0))

    return pl.pallas_call(
        picked_kernel,
        grid_spec=pltpu.PrefetchScalarGridSpec(
            num_scalar_prefetch=1,
            grid=(1,),
            in_specs=[block(f) for f in range(number)],
            out_specs=pl.BlockSpec((number, 128, 256), lambda t, m: (0, 0, 0)),
        ),
        out_shape=jax.ShapeDtypeStruct((number, 128, 256), BF16),
        cost_estimate=SMALL,
        name="picked",
    )(meta, *[image] * number)


def last_energy_kernel(meta_ref, first, swapped, before, image, out, lines):
    lines[0:64] = before[...]
    lines[64:128] = jnp.zeros((64, 128), F32)
    for f in range(swapped.shape[0]):
        place = meta_ref[2 * SLOTS + first + f]
        line = jnp.sum(swapped[f].astype(F32) * image[f].astype(F32), axis=0, keepdims=True)
        lines[pl.ds(place, 1), :] = line[:, :128] + line[:, 128:]
    out[...] = jnp.sum(lines[...].T, axis=0, keepdims=True)[:, :64] * (1.0 / 256)


def make_last_energy(meta, first, swapped, image, before):
    vmem = pl.BlockSpec(memory_space=pltpu.VMEM)
    return pl.pallas_call(
        lambda meta_ref, *refs: last_energy_kernel(meta_ref, first, *refs),
        in_specs=[SMEM, vmem, vmem, vmem],
        out_specs=vmem,
        out_shape=jax.ShapeDtypeStruct((1, 64), F32),
        scratch_shapes=[pltpu.VMEM((128, 128), F32)],
        cost_estimate=SMALL,
        compiler_params=params(16),
        name="energies",
    )(meta, swapped, before, image)


def taken_kernel(whole, out, done):
    copies = []
    for part in range(4):
        rows = pl.ds(part * (FIRST // 4), FIRST // 4)
        copies.append(pltpu.make_async_copy(whole.at[rows], out.at[rows], done.at[part]))
        copies[-1].start()
    for copy in copies:
        copy.wait()


def make_taken(density):
    return pl.pallas_call(
        taken_kernel,
        in_specs=[ANY],
        out_specs=pl.BlockSpec(memory_space=pltpu.VMEM),
        out_shape=jax.ShapeDtypeStruct((FIRST, 128, 256), BF16),
        scratch_shapes=[pltpu.SemaphoreType.DMA((4,))],
        cost_estimate=SMALL,
        compiler_params=params(60),
        name="taken",
    )(density)


def along(array, axis, by):
    length = lax.axis_size(axis)
    return lax.ppermute(array, axis, [(i, i + by) for i in range(length) if 0 <= i + by < length])


def exchanged(array, axis):
    return lax.ppermute(array, axis, [(i, i ^ 1) for i in range(lax.axis_size(axis))])


def body(density, core_hamiltonian, coulomb_kernel, esp_kernel, contacts, coupling, partner):
    own = lax.axis_index("frag").astype(jnp.int32).reshape(1)
    inner = lax.axis_index("inner").astype(jnp.int32).reshape(1)
    first = exchanged(make_taken(density), "frag")
    other = exchanged(density, "inner")
    meta, sent, weights = make_index(own, contacts.T, coupling.T, partner)
    outgoing = make_outgoing(meta, inner, sent, esp_kernel, density, other)
    arrived = [along(block, "frag", by) for block, by in zip(outgoing, OFFSETS)]
    image, sums, part = make_local(
        inner, density, other, esp_kernel, coulomb_kernel, core_hamiltonian, weights, outgoing[-1]
    )
    second = exchanged(part, "frag")
    lines = make_energy(meta, 0, first, image, jnp.zeros((64, 128), F32))
    low, high = make_fock(meta, 32 - inner * 32, sums, arrived, lines, SHARES)
    (stay,) = make_fock(meta, inner * 32, sums, arrived, lines, (sum(SHARES),))
    low, high = exchanged(low, "inner"), exchanged(high, "inner")
    fock, new_density, part, lines = make_pure(inner, stay, low, high, density, lines)
    third = exchanged(part, "frag")
    picked = make_picked(meta, FIRST + SECOND, third.shape[0], image)
    lines = make_energy(meta, FIRST, second, image, lines)
    partial = make_last_energy(meta, FIRST + SECOND, third, picked, lines)
    energy = (partial + exchanged(partial, "inner")).reshape(64)
    return (fock, new_density, energy)


def solution(mesh):
    rows = P("frag", "inner", None)
    whole = P(("frag", "inner"), None, None)
    return jax.shard_map(
        body,
        mesh=mesh,
        in_specs=(rows, rows, rows, rows, P(), P("frag", None), P("frag")),
        out_specs=(whole, whole, P("frag")),
        check_vma=False,
    )
```
